32 devices in a mesh: ha: 8 (over z, y), ba: 4 (over x, core).
Axes of the slice: x: 2, y: 2, z: 4, core: 2. Of those that a mesh axis runs over, the one named last changes fastest.
Arguments:
- images: bfloat16 [12, 16, 72, 2048], P('ba', 'ha'), may hold values from -6 to 6
- w_reduce: bfloat16 [2, 2048, 512], replicated, may hold values from -0.125 to 0.125
- w_spatial: bfloat16 [2, 3, 3, 512, 512], replicated, may hold values from -0.09375 to 0.09375
- w_expand: bfloat16 [2, 512, 2048], replicated, may hold values from -0.25 to 0.25
- gain_mid: float32 [2, 2, 512], replicated, may hold values from 0.5 to 1.5
- bias_mid: float32 [2, 2, 512], replicated, may hold values from -3 to 3
- gain_out: float32 [2, 2048], replicated, may hold values from 0.5 to 1.5
- bias_out: float32 [2, 2048], replicated, may hold values from -3 to 3
- w_heads: bfloat16 [2048, 768], replicated, may hold values from -0.125 to 0.125
- targets: int32 [12, 16, 72, 768], P('ba', 'ha'), may hold values from -8 to 8
- thresholds: int32 [12, 16, 72], P('ba', 'ha'), may hold values from 0 to 1000
Outputs:
- activations: bfloat16 [12, 16, 72, 2048], P('ba', 'ha')
- input_grad: float32 [12, 16, 72, 2048], P('ba', 'ha')
- grad_reduce: float32 [2, 2048, 512], P(None, 'ha', 'ba')
- grad_spatial: float32 [2, 3, 3, 512, 512], P(None, None, None, 'ba', 'ha')
- grad_expand: float32 [2, 512, 2048], P(None, 'ba', 'ha')
- grad_gain_mid: float32 [2, 2, 512], replicated
- grad_bias_mid: float32 [2, 2, 512], replicated
- output_gain_gradient: float32 [2, 2048], replicated
- grad_bias_out: float32 [2, 2048], replicated
- grad_heads: float32 [2048, 768], P('ha', 'ba')
The draws below stay inside these ranges and needn't reach their ends.
All inputs are finite; a program needn't handle non-finite values.
Results may differ from the reference program's by a relative error of at most 0.025.
Values may be sent and summed in bfloat16 or wider, within the bound.
No kernel may reach another device: no remote copies, remote signals or barrier semaphores. Data moves between devices by JAX's collectives and lax.ppermute only.
A program may use at most 256 MiB of HBM per device.

```python
import math
import jax
import jax.numpy as jnp
from jax import lax

C = 2048
M = 512
HEAD = 256
TASKS = 3
W = 72
IMAGES = 12
HEIGHT = 16


def touch_ends(result, own_key, smallest, top_value):
    index_at = [jax.random.randint(jax.random.fold_in(own_key, axis), (), 0, length) for axis, length in enumerate(result.shape)]
    widest = result.shape.index(max(result.shape))
    neighbour = index_at[:widest] + [(index_at[widest] + 1) % result.shape[widest]] + index_at[widest + 1:]
    return result.at[tuple(index_at)].set(smallest).at[tuple(neighbour)].set(top_value)


def shard_levels(stream_key, shape, split, least, high):
    level, own = 1.0, jax.random.fold_in(stream_key, 6)
    for position, shards_of in split:
        heights = jnp.exp(jax.random.uniform(jax.random.fold_in(own, position), (shards_of,), jnp.float32, least / len(split), high / len(split)))
        level = level * jnp.repeat(heights, shape[position] // shards_of).reshape([-1 if axis == position else 1 for axis in range(len(shape))])
    return level


def centred(stream_key, dims, deviation, most, pieces=(), kind=jnp.bfloat16):
    result = deviation * jax.random.normal(stream_key, dims, jnp.float32)
    if pieces:
        result = result * shard_levels(stream_key, dims, pieces, -0.22, 0.18)
    return jnp.clip(result, -most, most).astype(kind)


def setup_inputs(seed: int = 0) -> dict:
    splits = jax.random.split(jax.random.key(seed), 12)
    return {
        "images": centred(splits[0], (IMAGES, HEIGHT, W, C), 1.0, 6.0, ((0, 4), (1, 8))),
        "w_reduce": centred(splits[1], (2, C, M), C ** -0.5, 0.125),
        "w_spatial": centred(splits[2], (2, 3, 3, M, M), (9 * M) ** -0.5, 0.09375),
        "w_expand": centred(splits[3], (2, M, C), M ** -0.5, 0.25),
        "gain_mid": jnp.clip(1.0 + 0.1 * jax.random.normal(splits[4], (2, 2, M), jnp.float32), 0.5, 1.5),
        "bias_mid": centred(splits[5], (2, 2, M), 0.5, 3.0, (), jnp.float32),
        "gain_out": jnp.clip(1.0 + 0.1 * jax.random.normal(splits[6], (2, C), jnp.float32), 0.5, 1.5),
        "bias_out": centred(splits[7], (2, C), 0.5, 3.0, (), jnp.float32),
        "w_heads": centred(splits[8], (C, TASKS * HEAD), C ** -0.5, 0.125),
        "targets": touch_ends(jax.random.randint(splits[9], (IMAGES, HEIGHT, W, TASKS * HEAD), -8, 9), jax.random.fold_in(splits[9], 1), -8, 8).astype(jnp.int32),
        "thresholds": touch_ends(jax.random.randint(splits[10], (IMAGES, HEIGHT, W), 0, 1001), jax.random.fold_in(splits[10], 1), 0, 1000).astype(jnp.int32),
    }


EPS = 1e-05
SIGN_WIDTH = 0.1
TEMPER = 0.1
ABS_EPS = 0.01

@jax.custom_vjp
def low(v):
    return lax.optimization_barrier(v.astype(jnp.bfloat16)).astype(jnp.float32)

@jax.custom_vjp
def low_back(v):
    return v

def low_keep(v):
    return (low(v), None)

def low_pass(kept, grad):
    return (grad,)

def back_keep(v):
    return (v, None)

def back_low(kept, grad):
    return (low(grad),)
low.defvjp(low_keep, low_pass)
low_back.defvjp(back_keep, back_low)

def pointwise(a, w):
    return jnp.einsum('nhwc,cm->nhwm', a, w, precision=lax.Precision.HIGHEST)

def spatial(a, w):
    return lax.conv_general_dilated(a, w, (1, 1), ((1, 1), (1, 1)), dimension_numbers=('NHWC', 'HWIO', 'NHWC'), precision=lax.Precision.HIGHEST)

def normalize(z, gain, bias):
    mean = lax.optimization_barrier(jnp.mean(z, axis=(0, 1, 2)))
    var = lax.optimization_barrier(jnp.mean(jnp.square(z - mean), axis=(0, 1, 2)))
    return (z - mean) * lax.rsqrt(var + EPS) * gain + bias

def smooth(v):
    return jax.nn.gelu(v, approximate=False)

def block(inputs, w_one, w_two, w_three, gains, biases, gain_last, bias_last):
    z_one = low_back(pointwise(inputs, w_one))
    act_one = low(smooth(normalize(z_one, gains[0], biases[0])))
    z_two = low_back(spatial(act_one, w_two))
    act_two = low(smooth(normalize(z_two, gains[1], biases[1])))
    z_three = low_back(pointwise(act_two, w_three))
    return low(smooth(normalize(z_three, gain_last, bias_last) + inputs))

def trunk(images, w_reduce, w_spatial, w_expand, gain_mid, bias_mid, gain_out, bias_out):
    state = images
    for layer in range(2):
        state = block(state, w_reduce[layer], w_spatial[layer], w_expand[layer], gain_mid[layer], bias_mid[layer], gain_out[layer], bias_out[layer])
    return state

def heads(state, w_heads):
    return low_back(pointwise(state, w_heads))

def graddrop(parts, level, amplify):
    scaled = [p * amplify for p in parts]
    agree = scaled[0] + scaled[1] + scaled[2]
    spread = jnp.sqrt(scaled[0] * scaled[0] + ABS_EPS) + jnp.sqrt(scaled[1] * scaled[1] + ABS_EPS) + jnp.sqrt(scaled[2] * scaled[2] + ABS_EPS)
    purity = 0.5 * (1.0 + agree / spread)
    keep = jax.nn.sigmoid((purity - level) / TEMPER)
    merged = jnp.zeros_like(parts[0])
    for part, lifted in zip(parts, scaled):
        positive = jax.nn.sigmoid(lifted / SIGN_WIDTH)
        merged = merged + part * (keep * positive + (1.0 - keep) * (1.0 - positive))
    return merged

def reference(images, w_reduce, w_spatial, w_expand, gain_mid, bias_mid, gain_out, bias_out, w_heads, targets, thresholds):
    f32 = jnp.float32
    floats = (images.astype(f32), w_reduce.astype(f32), w_spatial.astype(f32), w_expand.astype(f32), gain_mid.astype(f32), bias_mid.astype(f32), gain_out.astype(f32), bias_out.astype(f32))
    state, trunk_back = jax.vjp(trunk, *floats)
    pred, head_back = jax.vjp(heads, state, w_heads.astype(f32))
    pixels = images.shape[0] * images.shape[1] * images.shape[2]
    cot = (pred - targets.astype(f32) * 0.25) * (1.0 / math.sqrt(pixels))
    grad_heads = head_back(cot)[1]
    task = jnp.arange(pred.shape[-1], dtype=jnp.int32) // HEAD
    parts = [head_back(cot * (task == t).astype(f32))[0] for t in range(3)]
    level = thresholds.astype(f32)[..., None] * 0.001
    merged = graddrop(parts, level, math.sqrt(pixels))
    grads = trunk_back(merged)
    return (state.astype(jnp.bfloat16), grads[0], grads[1], grads[2], grads[3], grads[4], grads[5], grads[6], grads[7], grad_heads)
```

```python
import math

import jax
import jax.numpy as jnp
from jax import lax
from jax.sharding import PartitionSpec as P

EPS = 1e-05
SIGN_WIDTH = 0.1
TEMPER = 0.1
ABS_EPS = 0.01


def padded_2(x, sides, width):
    for axis, dim in sides:
        devices, length = (lax.axis_size(axis), x.shape[dim])
        up = [(i, (i + 1) % devices) for i in range(devices - 1)]
        down = [(j, i) for i, j in up]
        last = lax.slice_in_dim(x, length - width, length, axis=dim)
        leading = lax.slice_in_dim(x, 0, width, axis=dim)
        before = lax.ppermute(last, axis, up)
        after = lax.ppermute(leading, axis, down)
        x = jnp.concatenate([before, x, after], axis=dim)
    return x


def smooth(v):
    return jax.nn.gelu(v, approximate=False)


def smooth_back(pre, grad):
    pull = jax.vjp(smooth, pre)[1]
    return pull(grad)[0]


def outer(left, right):
    return lax.dot_general(
        left, right, (((0,), (0,)), ((), ())), preferred_element_type=jnp.float32
    )


def against(left, right):
    return lax.dot_general(
        left, right, (((1,), (1,)), ((), ())), preferred_element_type=jnp.float32
    )


def spatial(framed, weight):
    return lax.conv_general_dilated(
        framed,
        weight,
        (1, 1),
        ((0, 0), (1, 1)),
        dimension_numbers=("NHWC", "HWIO", "NHWC"),
        preferred_element_type=jnp.float32,
    )


BOTH = ("ha", "ba")


def spread(x, groups=None, count=None):
    count = count or lax.axis_size(BOTH)
    copies = jnp.broadcast_to(x[None], (count,) + x.shape)
    return lax.all_to_all(copies, BOTH, 0, 0, tiled=True, axis_index_groups=groups)


def shared(x, merge):
    if x.shape[1] <= 512:
        return merge(spread(x))
    devices, cores = lax.axis_size(BOTH), lax.axis_size("ba")
    swap = [(i, i ^ 1) for i in range(cores)]
    half = x.shape[1] // 2
    core = lax.axis_index("ba") % 2
    own = lax.dynamic_slice_in_dim(x, core * half, half, 1)
    other = lax.dynamic_slice_in_dim(x, (1 - core) * half, half, 1)
    pair = jnp.stack([own, lax.ppermute(other, "ba", swap)])
    pair = jnp.where(core == 0, pair, pair[::-1])
    groups = [list(range(c, devices, 2)) for c in range(2)]
    own = merge(spread(merge(pair), groups, devices // 2))
    other = lax.ppermute(own, "ba", swap)
    first, last = jnp.where(core == 0, own, other), jnp.where(core == 0, other, own)
    return jnp.concatenate([first, last], 1)


def merge_moments(stack):
    means, squares = stack[:, 0], stack[:, 1]
    mean = jnp.mean(means, 0)
    off = means - mean
    return jnp.stack([mean, jnp.mean(squares, 0) + jnp.mean(off * off, 0)])


def merge_sums(stack):
    return jnp.sum(stack, 0)


def normalize(z_value, total):
    own = jnp.mean(z_value, 0)
    centred = z_value - own
    mean, var = shared(jnp.stack([own, jnp.mean(centred * centred, 0)]), merge_moments)
    scale = lax.rsqrt(var + EPS)
    return ((z_value - mean) * scale, scale)


def norm_back(grad, hatted, scale, gain, total):
    d_bias, d_gain = shared(jnp.stack([jnp.sum(grad, 0), jnp.sum(grad * hatted, 0)]), merge_sums)
    d_value = gain * scale * (grad - d_bias / total - hatted * d_gain / total)
    return (d_value.astype(jnp.bfloat16), d_gain, d_bias)


def forward_block(inputs, w_one, w_two, w_three, gains, biases, gain_last, bias_last, shape, total):
    count, rows, width = shape
    z_one = jnp.dot(inputs, w_one, preferred_element_type=jnp.float32)
    hat_one, scale_one = normalize(z_one, total)
    pre_one = hat_one * gains[0] + biases[0]
    act_one = smooth(pre_one).astype(jnp.bfloat16)
    framed = padded_2(act_one.reshape(count, rows, width, -1), (("ha", 1),), 1)
    z_two = spatial(framed, w_two).reshape(-1, w_two.shape[3])
    hat_two, scale_two = normalize(z_two, total)
    pre_two = hat_two * gains[1] + biases[1]
    act_two = smooth(pre_two).astype(jnp.bfloat16)
    z_three = jnp.dot(act_two, w_three, preferred_element_type=jnp.float32)
    hat_three, scale_three = normalize(z_three, total)
    summed = hat_three * gain_last + bias_last + inputs.astype(jnp.float32)
    result = smooth(summed).astype(jnp.bfloat16)
    return {
        "inputs": inputs,
        "hat_one": hat_one,
        "scale_one": scale_one,
        "pre_one": pre_one,
        "framed": framed,
        "hat_two": hat_two,
        "scale_two": scale_two,
        "pre_two": pre_two,
        "act_two": act_two,
        "hat_three": hat_three,
        "scale_three": scale_three,
        "summed": summed,
        "result": result,
    }


def block_backward_pass(saved, grad_out, w_one, w_two, w_three, gains, gain_last, shape, total):
    count, rows, width = shape
    d_sum = smooth_back(saved["summed"], grad_out)
    dz_three, dg_three, db_three = norm_back(
        d_sum, saved["hat_three"], saved["scale_three"], gain_last, total
    )
    dw_three = outer(saved["act_two"], dz_three)
    d_act_two = against(dz_three, w_three)
    d_pre_two = smooth_back(saved["pre_two"], d_act_two)
    dz_two, dg_two, db_two = norm_back(
        d_pre_two, saved["hat_two"], saved["scale_two"], gains[1], total
    )
    dz_image = dz_two.reshape(count, rows, width, -1)
    framed_grad = padded_2(dz_image, (("ha", 1),), 1)
    flipped = jnp.transpose(w_two[::-1, ::-1], (0, 1, 3, 2))
    d_act_one = spatial(framed_grad, flipped).reshape(-1, w_two.shape[2])
    padded = jnp.pad(saved["framed"], ((0, 0), (0, 0), (1, 1), (0, 0)))
    dw_two = jnp.stack(
        [
            jnp.stack(
                [
                    jnp.einsum(
                        "irwm,irwn->mn",
                        padded[:, kh : kh + rows, kw : kw + width, :],
                        dz_image,
                        preferred_element_type=jnp.float32,
                    )
                    for kw in range(3)
                ]
            )
            for kh in range(3)
        ]
    )
    d_pre_one = smooth_back(saved["pre_one"], d_act_one)
    dz_one, dg_one, db_one = norm_back(
        d_pre_one, saved["hat_one"], saved["scale_one"], gains[0], total
    )
    dw_one = outer(saved["inputs"], dz_one)
    d_inputs = d_sum + against(dz_one, w_one)
    return (
        d_inputs,
        (dw_one, dw_two, dw_three),
        jnp.stack([dg_one, dg_two]),
        jnp.stack([db_one, db_two]),
        dg_three,
        db_three,
    )


def graddrop(parts, level, amplify):
    scaled = [p * amplify for p in parts]
    agree = scaled[0] + scaled[1] + scaled[2]
    spread = (
        jnp.sqrt(scaled[0] * scaled[0] + ABS_EPS)
        + jnp.sqrt(scaled[1] * scaled[1] + ABS_EPS)
        + jnp.sqrt(scaled[2] * scaled[2] + ABS_EPS)
    )
    purity = 0.5 * (1.0 + agree / spread)
    keep = jax.nn.sigmoid((purity - level) / TEMPER)
    merged = jnp.zeros_like(parts[0])
    for part, lifted in zip(parts, scaled):
        positive = jax.nn.sigmoid(lifted / SIGN_WIDTH)
        merged = merged + part * (keep * positive + (1.0 - keep) * (1.0 - positive))
    return merged


def scatter_sum(x, row_axis, column_axis):
    lead, rows, columns = x.shape
    bits = {axis: lax.axis_size(axis).bit_length() - 1 for axis in BOTH}
    row_bits, column_bits = bits[row_axis], bits[column_axis]
    x = x.astype(jnp.bfloat16).reshape(
        (lead,) + (2,) * row_bits + (rows >> row_bits,) + (2,) * column_bits + (columns >> column_bits,)
    )
    place = {(row_axis, b): row_bits - b for b in range(row_bits)}
    place.update({(column_axis, b): 1 + row_bits + column_bits - b for b in range(column_bits)})
    order = [("ba", b) for b in range(bits["ba"])] + [("ha", b) for b in range(bits["ha"])]
    x = jnp.transpose(x, [place[key] for key in order] + [0, 1 + row_bits, 2 + row_bits + column_bits])
    for axis, bit in order:
        mine = (lax.axis_index(axis) >> bit) & 1
        swap = [(i, i ^ (1 << bit)) for i in range(lax.axis_size(axis))]
        kept = lax.dynamic_index_in_dim(x, mine, 0, keepdims=False)
        sent = lax.dynamic_index_in_dim(x, 1 - mine, 0, keepdims=False)
        got = lax.ppermute(sent, axis, swap)
        x = kept.astype(jnp.float32) + got.astype(jnp.float32)
        if (axis, bit) != order[-1]:
            x = x.astype(jnp.bfloat16)
    return x


def body(
    images,
    w_reduce,
    w_spatial,
    w_expand,
    gain_mid,
    bias_mid,
    gain_out,
    bias_out,
    w_heads,
    targets,
    thresholds,
):
    count, rows, width, chans = images.shape
    shape = (count, rows, width)
    total = count * rows * width * lax.axis_size("ha") * lax.axis_size("ba")
    head_cols = w_heads.shape[1] // 3
    state = images.reshape(-1, chans)
    kept = []
    for layer in range(2):
        saved = forward_block(
            state,
            w_reduce[layer],
            w_spatial[layer],
            w_expand[layer],
            gain_mid[layer],
            bias_mid[layer],
            gain_out[layer],
            bias_out[layer],
            shape,
            total,
        )
        kept.append(saved)
        state = saved["result"]
    pred = jnp.dot(state, w_heads, preferred_element_type=jnp.float32)
    wanted = targets.reshape(pred.shape).astype(jnp.float32) * 0.25
    cot = ((pred - wanted) * (1.0 / math.sqrt(total))).astype(jnp.bfloat16)
    head_grad = outer(state, cot)
    parts = [
        against(
            cot[:, t * head_cols : (t + 1) * head_cols],
            w_heads[:, t * head_cols : (t + 1) * head_cols],
        )
        for t in range(3)
    ]
    level = thresholds.reshape(-1, 1).astype(jnp.float32) * 0.001
    merged = graddrop(parts, level, math.sqrt(total))
    (
        late_block_gradient,
        late_gradient_list,
        late_middle_gain_gradient,
        late_middle_bias_gradient,
        late_output_gain_gradient,
        late_output_bias_gradient,
    ) = block_backward_pass(
        kept[1],
        merged,
        w_reduce[1],
        w_spatial[1],
        w_expand[1],
        gain_mid[1],
        gain_out[1],
        shape,
        total,
    )
    (
        early_block_gradient,
        early_gradient_list,
        early_middle_gain_gradient,
        early_middle_bias_gradient,
        early_output_gain_gradient,
        early_output_bias_gradient,
    ) = block_backward_pass(
        kept[0],
        late_block_gradient,
        w_reduce[0],
        w_spatial[0],
        w_expand[0],
        gain_mid[0],
        gain_out[0],
        shape,
        total,
    )
    both = (early_gradient_list, late_gradient_list)
    grad_reduce = jnp.stack([scatter_sum(g[0][None], "ha", "ba")[0] for g in both])
    grad_spatial = jnp.stack(
        [scatter_sum(g[1].reshape((9,) + g[1].shape[2:]), "ba", "ha") for g in both]
    )
    grad_spatial = grad_spatial.reshape((2, 3, 3) + grad_spatial.shape[2:])
    grad_expand = jnp.stack([scatter_sum(g[2][None], "ba", "ha")[0] for g in both])
    grad_heads = scatter_sum(head_grad[None], "ha", "ba")[0]
    input_grad = early_block_gradient.reshape(count, rows, width, chans)
    activations = state.reshape(count, rows, width, chans)
    grad_gain_mid = jnp.stack([early_middle_gain_gradient, late_middle_gain_gradient])
    grad_bias_mid = jnp.stack([early_middle_bias_gradient, late_middle_bias_gradient])
    output_gain_gradient = jnp.stack([early_output_gain_gradient, late_output_gain_gradient])
    grad_bias_out = jnp.stack([early_output_bias_gradient, late_output_bias_gradient])
    return (
        activations,
        input_grad,
        grad_reduce,
        grad_spatial,
        grad_expand,
        grad_gain_mid,
        grad_bias_mid,
        output_gain_gradient,
        grad_bias_out,
        grad_heads,
    )


def solution(mesh):
    return jax.shard_map(
        body,
        mesh=mesh,
        in_specs=(
            P("ba", "ha", None, None),
            P(),
            P(),
            P(),
            P(),
            P(),
            P(),
            P(),
            P(),
            P("ba", "ha", None, None),
            P("ba", "ha", None),
        ),
        out_specs=(
            P("ba", "ha", None, None),
            P("ba", "ha", None, None),
            P(None, "ha", "ba"),
            P(None, None, None, "ba", "ha"),
            P(None, "ba", "ha"),
            P(),
            P(),
            P(),
            P(),
            P("ha", "ba"),
        ),
        check_vma=False,
    )
```

```python
import functools
import math

import jax
import jax.numpy as jnp
from jax import lax
from jax.experimental import pallas as pl
from jax.experimental.pallas import tpu as pltpu
from jax.sharding import PartitionSpec as P

EPS = 1e-05
SIGN_WIDTH = 0.1
TEMPER = 0.1
ABS_EPS = 0.01
F32, BF16 = jnp.float32, jnp.bfloat16
BOTH = ("ha", "ba")
STEP = 16
BLOCK = 512
VMEM_LIMIT = 40 * 1024 * 1024


def phi(x):
    return 0.5 + 0.5 * lax.erf(x * math.sqrt(0.5))


def gelu(x):
    return x * phi(x)


def gelu_slope(x):
    return phi(x) + x * (1.0 / math.sqrt(2.0 * math.pi)) * jnp.exp(-0.5 * x * x)


def sigmoid(x):
    return 0.5 + 0.5 * jnp.tanh(0.5 * x)


def dot(a, b):
    return jnp.dot(a, b, preferred_element_type=F32)


def dot_nt(a, b):
    return lax.dot_general(a, b, (((1,), (1,)), ((), ())), preferred_element_type=F32)


def dot_tn(a, b):
    return lax.dot_general(a, b, (((0,), (0,)), ((), ())), preferred_element_type=F32)


def row_loop(count, body, init):
    def step(i, carry):
        return body(pl.ds(pl.multiple_of(i * STEP, STEP), STEP), carry)

    return lax.fori_loop(0, count // STEP, step, init)


def fold(x):
    return jnp.sum(x, 0, keepdims=True)


def moments(ref, columns):
    count = ref.shape[0]
    zero = jnp.zeros((STEP, columns.stop - columns.start), F32)
    total = row_loop(count, lambda rows, acc: acc + ref[rows, columns], zero)
    mean = fold(total) * (1.0 / count)

    def centred(rows, acc):
        off = ref[rows, columns] - mean
        return acc + off * off

    return mean, fold(row_loop(count, centred, zero)) * (1.0 / count)


def merged_moments(stack_ref):
    means, squares = stack_ref[:, 0, :], stack_ref[:, 1, :]
    share = 1.0 / means.shape[0]
    mean = fold(means) * share
    off = means - mean
    return mean, lax.rsqrt(fold(squares) * share + fold(off * off) * share + EPS)


def put_halves(core, pair, kept_ref, sent_ref):
    half = pair.shape[1] // 2
    low, high = pair[:, :half], pair[:, half:]
    kept_ref[...] = jnp.where(core == 0, low, high)
    sent_ref[...] = jnp.where(core == 0, high, low)


def take_halves(core, own_ref, other_ref):
    own, other = own_ref[...], other_ref[...]
    return jnp.concatenate([jnp.where(core == 0, own, other), jnp.where(core == 0, other, own)], 1)


def blocks(width, unit=1):
    size = min(max(BLOCK // unit, 1) * unit, width)
    return [slice(i, i + size) for i in range(0, width, size)]


def fetch(pairs, sems):
    copies = [pltpu.make_async_copy(src, dst, sems.at[i]) for i, (src, dst) in enumerate(pairs)]
    for copy in copies:
        copy.start()
    return copies


def edges(ref, first_ref, last_ref, shape):
    count, rows, width = shape
    for i in range(count):
        first_ref[i * width : (i + 1) * width, :] = ref[i * rows * width : (i * rows + 1) * width, :]
        last_ref[i * width : (i + 1) * width, :] = ref[((i + 1) * rows - 1) * width : (i + 1) * rows * width, :]


def reduce_kernel(layer, shape, u_ref, w_ref, z_ref, stat_ref, first_ref, last_ref, w_buf, sems):
    cuts = blocks(u_ref.shape[1])
    copies = fetch([(w_ref.at[layer, c, :], w_buf.at[c, :]) for c in cuts], sems)
    for i, c in enumerate(cuts):
        copies[i].wait()
        part = dot(u_ref[:, c], w_buf[c, :])
        z_ref[...] = part if i == 0 else z_ref[...] + part
    mean, square = moments(z_ref, slice(0, z_ref.shape[1]))
    stat_ref[0:1, :] = mean
    stat_ref[1:2, :] = square
    edges(z_ref, first_ref, last_ref, shape)


def fill_frame(frame_ref, shape, padded, sources, make):
    count, rows, width = shape
    prev, own, after = sources
    units = [(prev, i * width, i * padded, 0) for i in range(count)]
    units += [(after, i * width, ((rows + 1) * count + i) * padded, 1) for i in range(count)]
    units += [
        (own, (i * rows + r) * width, ((r + 1) * count + i) * padded, None) for i in range(count) for r in range(rows)
    ]
    lanes = frame_ref.shape[1] // 128

    def step(j, carry):
        columns = pl.ds(pl.multiple_of(j * 128, 128), 128)
        zero = jnp.zeros((padded - width, 128), F32)
        for source, start, target, side in units:
            value = make(source, pl.ds(start, width), columns, side)
            frame_ref[pl.ds(target, padded), columns] = jnp.concatenate([value, zero], 0).astype(BF16)
        return carry

    lax.fori_loop(0, lanes, step, 0)


def shifted_sum(acc_ref, shape, padded, shifts, out_ref, finish):
    count, rows, width = shape
    lanes = acc_ref.shape[2] // 128
    for j in range(lanes):
        columns = slice(j * 128, (j + 1) * 128)
        for i in range(count):
            for r in range(rows):
                base = 8 + (r * count + i) * padded
                total = None
                for k, shift in enumerate(shifts):
                    part = acc_ref[k, base + shift : base + shift + width, columns]
                    total = part if total is None else total + part
                start = (i * rows + r) * width
                out_ref[start : start + width, columns] = finish(total, slice(start, start + width), columns)


def spatial_kernel(
    layer, shape, padded,
    flags_ref, z_ref, prev_ref, next_ref, stack_ref, gain_ref, bias_ref, w_ref,
    frame_ref, out_ref, stat_ref, norm_ref, first_ref, last_ref, w_buf, acc_ref, sems,
):
    count, rows, width = shape
    copies = fetch([(w_ref.at[layer, :, kw], w_buf.at[kw]) for kw in range(3)], sems)
    mean, scale = merged_moments(stack_ref)
    norm_ref[0:1, :] = mean
    norm_ref[1:2, :] = scale

    def make(source, where, columns, side):
        m, s = norm_ref[0:1, columns], norm_ref[1:2, columns]
        value = gelu((source[where, columns] - m) * s * gain_ref[layer, 0:1, columns] + bias_ref[layer, 0:1, columns])
        return value if side is None else value * flags_ref[1 + side].astype(F32)

    fill_frame(frame_ref, shape, padded, (prev_ref, z_ref, next_ref), make)
    span = rows * count * padded
    acc_ref[:, 0:8, :] = jnp.zeros((3, 8, acc_ref.shape[2]), F32)
    acc_ref[:, 8 + span :, :] = jnp.zeros((3, 8, acc_ref.shape[2]), F32)
    for kw in range(3):
        copies[kw].wait()
        for kh in range(3):
            start = kh * count * padded
            part = dot(frame_ref[start : start + span, :], w_buf[kw, kh])
            acc_ref[kw, 8 : 8 + span, :] = part if kh == 0 else acc_ref[kw, 8 : 8 + span, :] + part
    shifted_sum(acc_ref, shape, padded, (-1, 0, 1), out_ref, lambda total, where, columns: total)
    mean, square = moments(out_ref, slice(0, out_ref.shape[1]))
    stat_ref[0:1, :] = mean
    stat_ref[1:2, :] = square
    edges(out_ref, first_ref, last_ref, shape)


def expand_kernel(
    layer, flags_ref, z_ref, stack_ref, gain_ref, bias_ref, w_ref,
    act_ref, out_ref, kept_ref, sent_ref, norm_ref, w_buf, sems,
):
    cuts = blocks(out_ref.shape[1])
    copies = fetch([(w_ref.at[layer, :, c], w_buf.at[:, c]) for c in cuts], sems)
    mean, scale = merged_moments(stack_ref)
    norm_ref[0:1, :] = mean
    norm_ref[1:2, :] = scale
    gain, bias = gain_ref[layer, 1:2, :], bias_ref[layer, 1:2, :]

    def step(rows, carry):
        act_ref[rows, :] = gelu((z_ref[rows, :] - mean) * scale * gain + bias).astype(BF16)
        return carry

    row_loop(z_ref.shape[0], step, 0)
    stats = []
    for i, c in enumerate(cuts):
        copies[i].wait()
        out_ref[:, c] = dot(act_ref[...], w_buf[:, c])
        stats.append(jnp.concatenate(moments(out_ref, c), 0))
    put_halves(flags_ref[0], jnp.concatenate(stats, 1), kept_ref, sent_ref)


def out_norm(flags_ref, own_ref, other_ref, norm_ref):
    pair = take_halves(flags_ref[0], own_ref, other_ref)
    norm_ref[0:1, :] = pair[0:1]
    norm_ref[1:2, :] = lax.rsqrt(pair[1:2] + EPS)


def summed(z_ref, u_ref, norm_ref, gain_ref, bias_ref, layer, rows, c):
    hat = (z_ref[rows, c] - norm_ref[0:1, c]) * norm_ref[1:2, c]
    return hat, hat * gain_ref[layer : layer + 1, c] + bias_ref[layer : layer + 1, c] + u_ref[rows, c].astype(F32)


def join_kernel(
    layer, shape, flags_ref, z_ref, u_ref, own_ref, other_ref, gain_ref, bias_ref, w_ref,
    state_ref, out_ref, stat_ref, first_ref, last_ref, norm_ref, w_buf, sems,
):
    cuts = blocks(z_ref.shape[1])
    copies = fetch([(w_ref.at[layer + 1, c, :], w_buf.at[c, :]) for c in cuts], sems)
    out_norm(flags_ref, own_ref, other_ref, norm_ref)
    for i, c in enumerate(cuts):

        def step(rows, carry, c=c):
            state_ref[rows, c] = gelu(
                summed(z_ref, u_ref, norm_ref, gain_ref, bias_ref, layer, rows, c)[1]
            ).astype(BF16)
            return carry

        row_loop(z_ref.shape[0], step, 0)
        copies[i].wait()
        part = dot(state_ref[:, c], w_buf[c, :])
        out_ref[...] = part if i == 0 else out_ref[...] + part
    mean, square = moments(out_ref, slice(0, out_ref.shape[1]))
    stat_ref[0:1, :] = mean
    stat_ref[1:2, :] = square
    edges(out_ref, first_ref, last_ref, shape)


def heads_kernel(
    layer, total, flags_ref, z_ref, u_ref, own_ref, other_ref, gain_ref, bias_ref, w_ref, want_ref, level_ref,
    state_ref, cot_ref, grad_ref, kept_ref, sent_ref, norm_ref, w_buf, pred_ref, part_ref, sems,
):
    pixels = z_ref.shape[0]
    cuts = blocks(z_ref.shape[1])
    copies = fetch([(w_ref.at[c, :], w_buf.at[c, :]) for c in cuts], sems)
    out_norm(flags_ref, own_ref, other_ref, norm_ref)
    for i, c in enumerate(cuts):

        def step(rows, carry, c=c):
            state_ref[rows, c] = gelu(
                summed(z_ref, u_ref, norm_ref, gain_ref, bias_ref, layer, rows, c)[1]
            ).astype(BF16)
            return carry

        row_loop(pixels, step, 0)
        copies[i].wait()
        part = dot(state_ref[:, c], w_buf[c, :])
        pred_ref[...] = part if i == 0 else pred_ref[...] + part

    def error(rows, carry):
        wanted = want_ref[rows, :].astype(F32) * 0.25
        cot_ref[rows, :] = ((pred_ref[rows, :] - wanted) * (1.0 / math.sqrt(total))).astype(BF16)
        return carry

    row_loop(pixels, error, 0)
    head = cot_ref.shape[1] // 3
    amplify = math.sqrt(total)
    stats = []
    for c in cuts:
        for t in range(3):
            columns = slice(t * head, (t + 1) * head)
            part_ref[t] = dot_nt(cot_ref[:, columns], w_buf[c, columns])

        def drop(rows, carry, c=c):
            parts = [part_ref[t, rows, :] for t in range(3)]
            scaled = [p * amplify for p in parts]
            spread = sum(jnp.sqrt(h * h + ABS_EPS) for h in scaled)
            purity = 0.5 * (1.0 + (scaled[0] + scaled[1] + scaled[2]) / spread)
            keep = sigmoid((purity - level_ref[rows, :]) * (1.0 / TEMPER))
            merged = None
            for p, h in zip(parts, scaled):
                positive = sigmoid(h * (1.0 / SIGN_WIDTH))
                term = p * (keep * positive + (1.0 - keep) * (1.0 - positive))
                merged = term if merged is None else merged + term
            hat, pre = summed(z_ref, u_ref, norm_ref, gain_ref, bias_ref, layer, rows, c)
            grad = gelu_slope(pre) * merged
            grad_ref[rows, c] = grad
            return carry[0] + grad, carry[1] + grad * hat

        zero = jnp.zeros((STEP, c.stop - c.start), F32)
        sums = row_loop(pixels, drop, (zero, zero))
        stats.append(jnp.concatenate([fold(s) for s in sums], 0))
    put_halves(flags_ref[0], jnp.concatenate(stats, 1), kept_ref, sent_ref)


def expand_back_kernel(
    layer, total, flags_ref, grad_ref, z_out_ref, norm_out_ref, own_ref, other_ref, gain_out_ref,
    z_ref, norm_ref, gain_ref, bias_ref, w_ref,
    dz_ref, pre_ref, stat_ref, sums_ref, first_ref, last_ref, w_buf, acc_ref, sems, *, shape,
):
    pixels = z_ref.shape[0]
    cuts = blocks(grad_ref.shape[1])
    copies = fetch([(w_ref.at[layer, :, c], w_buf.at[:, c]) for c in cuts], sems)
    sums_ref[...] = take_halves(flags_ref[0], own_ref, other_ref)
    for i, c in enumerate(cuts):
        mean, scale = norm_out_ref[0:1, c], norm_out_ref[1:2, c]
        d_bias, d_gain = sums_ref[0:1, c] * (1.0 / total), sums_ref[1:2, c] * (1.0 / total)
        factor = gain_out_ref[layer : layer + 1, c] * scale

        def step(rows, carry, c=c, mean=mean, scale=scale, d_bias=d_bias, d_gain=d_gain, factor=factor):
            hat = (z_out_ref[rows, c] - mean) * scale
            dz_ref[rows, c] = (factor * (grad_ref[rows, c] - d_bias - hat * d_gain)).astype(BF16)
            return carry

        row_loop(pixels, step, 0)
        copies[i].wait()
        part = dot_nt(dz_ref[:, c], w_buf[:, c])
        acc_ref[...] = part if i == 0 else acc_ref[...] + part
    mean, scale = norm_ref[0:1, :], norm_ref[1:2, :]
    gain, bias = gain_ref[layer, 1:2, :], bias_ref[layer, 1:2, :]

    def slope(rows, carry):
        hat = (z_ref[rows, :] - mean) * scale
        grad = gelu_slope(hat * gain + bias) * acc_ref[rows, :]
        pre_ref[rows, :] = grad
        return carry[0] + grad, carry[1] + grad * hat

    zero = jnp.zeros((STEP, z_ref.shape[1]), F32)
    s_bias, s_gain = row_loop(pixels, slope, (zero, zero))
    stat_ref[0:1, :] = fold(s_bias)
    stat_ref[1:2, :] = fold(s_gain)
    edges(pre_ref, first_ref, last_ref, shape)


def spatial_back_kernel(
    layer, total, shape, padded, flags_ref, grad_ref, grad_prev_ref, grad_next_ref, z_ref, z_prev_ref, z_next_ref,
    norm_ref, stack_ref, gain_ref, bias_ref, z_in_ref, norm_in_ref, w_ref,
    frame_ref, pre_ref, stat_ref, sums_ref, w_buf, acc_ref, sems,
):
    count, rows, width = shape
    copies = fetch([(w_ref.at[layer, :, kw], w_buf.at[kw]) for kw in range(3)], sems)
    sums_ref[0:1, :] = fold(stack_ref[:, 0, :])
    sums_ref[1:2, :] = fold(stack_ref[:, 1, :])

    def make(source, where, columns, side):
        scale = norm_ref[1:2, columns]
        hat = (source[1][where, columns] - norm_ref[0:1, columns]) * scale
        d_bias, d_gain = sums_ref[0:1, columns] * (1.0 / total), sums_ref[1:2, columns] * (1.0 / total)
        value = gain_ref[layer, 1:2, columns] * scale * (source[0][where, columns] - d_bias - hat * d_gain)
        return value if side is None else value * flags_ref[1 + side].astype(F32)

    sources = ((grad_prev_ref, z_prev_ref), (grad_ref, z_ref), (grad_next_ref, z_next_ref))
    fill_frame(frame_ref, shape, padded, sources, make)
    span = rows * count * padded
    acc_ref[:, 0:8, :] = jnp.zeros((3, 8, acc_ref.shape[2]), F32)
    acc_ref[:, 8 + span :, :] = jnp.zeros((3, 8, acc_ref.shape[2]), F32)
    for kw in range(3):
        copies[kw].wait()
        for kh in range(3):
            start = (2 - kh) * count * padded
            part = dot_nt(frame_ref[start : start + span, :], w_buf[kw, kh])
            acc_ref[kw, 8 : 8 + span, :] = part if kh == 0 else acc_ref[kw, 8 : 8 + span, :] + part
    lanes = acc_ref.shape[2] // 128
    totals = [[None, None] for _ in range(lanes)]

    def finish(value, where, columns):
        hat = (z_in_ref[where, columns] - norm_in_ref[0:1, columns]) * norm_in_ref[1:2, columns]
        grad = gelu_slope(hat * gain_ref[layer, 0:1, columns] + bias_ref[layer, 0:1, columns]) * value
        keep = totals[columns.start // 128]
        for k, term in enumerate((grad, grad * hat)):
            keep[k] = fold(term) if keep[k] is None else keep[k] + fold(term)
        return grad

    shifted_sum(acc_ref, shape, padded, (1, 0, -1), pre_ref, finish)
    for j in range(lanes):
        for k in range(2):
            stat_ref[k : k + 1, j * 128 : (j + 1) * 128] = totals[j][k]


def reduce_back_start(layer, total, grad_ref, z_ref, norm_ref, stack_ref, gain_ref, dz_ref, sums_ref):
    sums_ref[0:1, :] = fold(stack_ref[:, 0, :])
    sums_ref[1:2, :] = fold(stack_ref[:, 1, :])
    mean, scale = norm_ref[0:1, :], norm_ref[1:2, :]
    d_bias, d_gain = sums_ref[0:1, :] * (1.0 / total), sums_ref[1:2, :] * (1.0 / total)
    factor = gain_ref[layer, 0:1, :] * scale

    def step(rows, carry):
        hat = (z_ref[rows, :] - mean) * scale
        dz_ref[rows, :] = (factor * (grad_ref[rows, :] - d_bias - hat * d_gain)).astype(BF16)
        return carry

    row_loop(z_ref.shape[0], step, 0)


def reduce_back_kernel(
    layer, total, flags_ref, grad_ref, z_ref, norm_ref, stack_ref, gain_ref, w_ref, out_grad_ref,
    z_out_ref, u_ref, norm_out_ref, gain_out_ref, bias_out_ref,
    dz_ref, sums_ref, next_ref, kept_ref, sent_ref, w_buf, part_ref, sems,
):
    cuts = blocks(out_grad_ref.shape[1])
    copies = fetch([(w_ref.at[layer, c, :], w_buf.at[c, :]) for c in cuts], sems)
    reduce_back_start(layer, total, grad_ref, z_ref, norm_ref, stack_ref, gain_ref, dz_ref, sums_ref)
    stats = []
    for i, c in enumerate(cuts):
        copies[i].wait()
        part_ref[...] = dot_nt(dz_ref[...], w_buf[c, :])

        def slope(rows, carry, c=c):
            hat, pre = summed(z_out_ref, u_ref, norm_out_ref, gain_out_ref, bias_out_ref, layer - 1, rows, c)
            grad = gelu_slope(pre) * (out_grad_ref[rows, c] + part_ref[rows, :])
            next_ref[rows, c] = grad
            return carry[0] + grad, carry[1] + grad * hat

        zero = jnp.zeros((STEP, c.stop - c.start), F32)
        sums = row_loop(z_ref.shape[0], slope, (zero, zero))
        stats.append(jnp.concatenate([fold(s) for s in sums], 0))
    put_halves(flags_ref[0], jnp.concatenate(stats, 1), kept_ref, sent_ref)


def input_kernel(
    layer, total, grad_ref, z_ref, norm_ref, stack_ref, gain_ref, dz_ref, sums_ref
):
    reduce_back_start(layer, total, grad_ref, z_ref, norm_ref, stack_ref, gain_ref, dz_ref, sums_ref)


def input_grad_kernel(layer, dz_ref, out_grad_ref, w_ref, next_ref, w_buf, sems):
    cuts = blocks(out_grad_ref.shape[1])
    copies = fetch([(w_ref.at[layer, c, :], w_buf.at[c, :]) for c in cuts], sems)
    for i, c in enumerate(cuts):
        copies[i].wait()
        next_ref[:, c] = out_grad_ref[:, c] + dot_nt(dz_ref[...], w_buf[c, :])


def store_tiles(out_ref, value, row, column, lead, places):
    if places is None:
        out_ref[lead, row : row + value.shape[0], column : column + value.shape[1]] = value.astype(BF16)
        return
    height, width = out_ref.shape[-2:]
    for i in range(0, value.shape[0], height):
        for j in range(0, value.shape[1], width):
            place = places[(row + i) // height][(column + j) // width]
            out_ref[place + (lead,)] = value[i : i + height, j : j + width].astype(BF16)


def outer_kernel(places, left_ref, right_ref, out_ref):
    height, width = out_ref.shape[-2:] if places else (1, 1)
    for a in blocks(left_ref.shape[1], height):
        for b in blocks(right_ref.shape[1], width):
            store_tiles(out_ref, dot_tn(left_ref[:, a], right_ref[:, b]), a.start, b.start, 0, places)


def spatial_outer_kernel(places, shape, padded, grad_ref, frame_ref, out_ref, line_ref, moved_ref):
    count, rows, width = shape
    span = rows * count * padded
    start = count * padded
    line_ref[0:8, :] = jnp.zeros((8, line_ref.shape[1]), F32)
    line_ref[8 + span :, :] = jnp.zeros((8, line_ref.shape[1]), F32)
    line_ref[8 : 8 + span, :] = grad_ref[start : start + span, :].astype(F32)
    for kw in range(3):
        for b in range(0, span, padded):
            for c in range(0, line_ref.shape[1], 128):
                moved_ref[b : b + padded, c : c + 128] = line_ref[
                    8 + b + 1 - kw : 8 + b + 1 - kw + padded, c : c + 128
                ].astype(BF16)
        for kh in range(3):
            at = kh * count * padded
            value = dot_tn(moved_ref[...], frame_ref[at : at + span, :])
            store_tiles(out_ref, value, 0, 0, 3 * kh + kw, places)


def shaped(shape, dtype=F32):
    return jax.ShapeDtypeStruct(shape, dtype)


WHOLE = pl.BlockSpec(memory_space=pltpu.VMEM)
HERE = pl.BlockSpec(memory_space=pl.ANY)
SCALARS = pl.BlockSpec(memory_space=pltpu.SMEM)


def call(name, kernel, specs, args, outs, scratch=(), flops=0):
    nbytes = sum(math.prod(o.shape) * o.dtype.itemsize for o in outs)
    kinds = {"v": WHOLE, "w": HERE, "s": SCALARS}
    return pl.pallas_call(
        kernel,
        out_shape=outs,
        in_specs=[kinds[s] for s in specs],
        out_specs=[WHOLE] * len(outs),
        scratch_shapes=list(scratch),
        compiler_params=pltpu.CompilerParams(vmem_limit_bytes=VMEM_LIMIT),
        cost_estimate=pl.CostEstimate(flops=flops, bytes_accessed=2 * nbytes, transcendentals=0),
        name=name,
    )(*args)


def spread(x, groups=None, count=None):
    count = count or lax.axis_size(BOTH)
    copies = jnp.broadcast_to(x[None], (count,) + x.shape)
    return lax.all_to_all(copies, BOTH, 0, 0, tiled=True, axis_index_groups=groups)


def merge_moments(stack):
    means, squares = stack[:, 0], stack[:, 1]
    mean = jnp.mean(means, 0)
    off = means - mean
    return jnp.stack([mean, jnp.mean(squares, 0) + jnp.mean(off * off, 0)])


def merge_sums(stack):
    return jnp.sum(stack, 0)


def share_halves(kept, sent, merge):
    devices, cores = lax.axis_size(BOTH), lax.axis_size("ba")
    swap = [(i, i ^ 1) for i in range(cores)]
    pair = merge(jnp.stack([kept, lax.ppermute(sent, "ba", swap)]))
    groups = [list(range(c, devices, 2)) for c in range(2)]
    own = merge(spread(pair, groups, devices // 2))
    return own, lax.ppermute(own, "ba", swap)


def neighbours(first, last):
    devices = lax.axis_size("ha")
    up = [(i, i + 1) for i in range(devices - 1)]
    down = [(j, i) for i, j in up]
    return lax.ppermute(last, "ha", up), lax.ppermute(first, "ha", down)


def halving_order():
    bits = {axis: lax.axis_size(axis).bit_length() - 1 for axis in BOTH}
    return [("ba", b) for b in range(bits["ba"])] + [("ha", b) for b in range(bits["ha"])]


def layout(lead, rows, columns, row_axis, column_axis):
    height, width = rows // lax.axis_size(row_axis), columns // lax.axis_size(column_axis)
    order = halving_order()
    if height % 16 or (width % 128 and width != columns):
        return shaped((lead, rows, columns), BF16), None
    places = [
        [
            tuple(((i if axis == row_axis else j) >> bit) & 1 for axis, bit in order)
            for j in range(lax.axis_size(column_axis))
        ]
        for i in range(lax.axis_size(row_axis))
    ]
    return shaped((2,) * len(order) + (lead, height, width), BF16), places


def tiles_of(x, row_axis, column_axis):
    lead, rows, columns = x.shape
    order = halving_order()
    row_bits = sum(axis == row_axis for axis, _ in order)
    column_bits = sum(axis == column_axis for axis, _ in order)
    x = x.reshape(
        (lead,) + (2,) * row_bits + (rows >> row_bits,) + (2,) * column_bits + (columns >> column_bits,)
    )
    place = {(row_axis, b): row_bits - b for b in range(row_bits)}
    place.update({(column_axis, b): 1 + row_bits + column_bits - b for b in range(column_bits)})
    return jnp.transpose(x, [place[key] for key in order] + [0, 1 + row_bits, 2 + row_bits + column_bits])


def scatter_sum(x, places, row_axis, column_axis):
    if places is None:
        x = tiles_of(x, row_axis, column_axis)
    order = halving_order()
    for axis, bit in order:
        mine = (lax.axis_index(axis) >> bit) & 1
        swap = [(i, i ^ (1 << bit)) for i in range(lax.axis_size(axis))]
        kept = lax.dynamic_index_in_dim(x, mine, 0, keepdims=False)
        sent = lax.dynamic_index_in_dim(x, 1 - mine, 0, keepdims=False)
        got = lax.ppermute(sent, axis, swap)
        x = kept.astype(F32) + got.astype(F32)
        if (axis, bit) != order[-1]:
            x = x.astype(BF16)
    return x


def outer(name, left, right, row_axis, column_axis):
    out, places = layout(1, left.shape[1], right.shape[1], row_axis, column_axis)
    flops = 2 * left.shape[0] * left.shape[1] * right.shape[1]
    x = call(name, functools.partial(outer_kernel, places), "vv", (left, right), [out], flops=flops)[0]
    return scatter_sum(x, places, row_axis, column_axis)[0]


def body(
    images, w_reduce, w_spatial, w_expand, gain_mid, bias_mid, gain_out, bias_out, w_heads, targets, thresholds
):
    count, rows, width, chans = images.shape
    shape = (count, rows, width)
    padded = (width // 16 + 1) * 16
    pixels = count * rows * width
    total = pixels * lax.axis_size(BOTH)
    mid = w_reduce.shape[2]
    head_columns = w_heads.shape[1]
    frame_rows, span = (rows + 2) * count * padded, rows * count * padded
    edge = shaped((count * width, mid))
    here = lax.axis_index("ha")
    flags = jnp.stack(
        [lax.axis_index("ba") % 2, (here > 0).astype(jnp.int32), (here < lax.axis_size("ha") - 1).astype(jnp.int32)]
    ).astype(jnp.int32)
    cuts = len(blocks(chans))
    sems = pltpu.SemaphoreType.DMA((cuts,))
    sems_3 = pltpu.SemaphoreType.DMA((3,))
    pair_mid, pair_out, half_out = shaped((2, mid)), shaped((2, chans)), shaped((2, chans // 2))
    mids, outs_f = shaped((pixels, mid)), shaped((pixels, chans))
    mids_b, outs_b = shaped((pixels, mid), BF16), shaped((pixels, chans), BF16)
    w_one, w_three = pltpu.VMEM((chans, mid), BF16), pltpu.VMEM((mid, chans), BF16)
    w_two, acc_two = pltpu.VMEM((3, 3, mid, mid), BF16), pltpu.VMEM((3, span + 16, mid), F32)
    small = 2 * pixels * chans * mid

    state = images.reshape(pixels, chans)
    kept = []
    z_one, stat, first, last = call(
        "reduce_0", functools.partial(reduce_kernel, 0, shape), "vw", (state, w_reduce),
        [mids, pair_mid, edge, edge], [w_one, sems], small,
    )
    for layer in range(2):
        prev, after = neighbours(first, last)
        stack = spread(stat)
        frame, z_two, stat, norm_one, first, last = call(
            f"spatial_{layer}", functools.partial(spatial_kernel, layer, shape, padded), "svvvvvvw",
            (flags, z_one, prev, after, stack, gain_mid, bias_mid, w_spatial),
            [shaped((frame_rows, mid), BF16), mids, pair_mid, pair_mid, edge, edge], [w_two, acc_two, sems_3], 10 * small // 4,
        )
        stack = spread(stat)
        z_two_edges = neighbours(first, last)
        act_two, z_three, keep, send, norm_two = call(
            f"expand_{layer}", functools.partial(expand_kernel, layer), "svvvvw",
            (flags, z_two, stack, gain_mid, bias_mid, w_expand),
            [mids_b, outs_f, half_out, half_out, pair_mid], [w_three, sems], small,
        )
        own, other = share_halves(keep, send, merge_moments)
        saved = dict(
            inputs=state, z_one=z_one, norm_one=norm_one, frame=frame, z_two=z_two, z_two_edges=z_two_edges,
            norm_two=norm_two, act_two=act_two, z_three=z_three,
        )
        kept.append(saved)
        if layer == 0:
            state, z_one, stat, first, last, saved["norm_three"] = call(
                "join", functools.partial(join_kernel, 0, shape), "svvvvvvw",
                (flags, z_three, state, own, other, gain_out, bias_out, w_reduce),
                [outs_b, mids, pair_mid, edge, edge, pair_out], [w_one, sems], small,
            )
    wanted = targets.reshape(pixels, head_columns)
    level = thresholds.reshape(pixels, 1).astype(F32) * 0.001
    state, cot, grad, keep, send, kept[1]["norm_three"] = call(
        "heads", functools.partial(heads_kernel, 1, total), "svvvvvvwvv",
        (flags, z_three, state, own, other, gain_out, bias_out, w_heads, wanted, level),
        [outs_b, shaped((pixels, head_columns), BF16), outs_f, half_out, half_out, pair_out],
        [
            pltpu.VMEM((chans, head_columns), BF16), pltpu.VMEM((pixels, head_columns), F32),
            pltpu.VMEM((3, pixels, min(BLOCK, chans)), F32), sems,
        ],
        3 * small,
    )
    activations = state
    grad_heads = outer("outer_heads", cot, activations, "ba", "ha").T

    reduce_grads, spatial_grads, expand_grads = [None, None], [None, None], [None, None]
    mid_sums, out_sums = [None, None], [None, None]
    for layer in (1, 0):
        k = kept[layer]
        own, other = share_halves(keep, send, merge_sums)
        dz_three, pre_two, stat, out_sums[layer], first, last = call(
            f"expand_back_{layer}", functools.partial(expand_back_kernel, layer, total, shape=shape), "svvvvvvvvvvw",
            (flags, grad, k["z_three"], k["norm_three"], own, other, gain_out, k["z_two"], k["norm_two"], gain_mid, bias_mid, w_expand),
            [outs_b, mids, pair_mid, pair_out, edge, edge], [w_three, pltpu.VMEM((pixels, mid), F32), sems], small,
        )
        grad_prev, grad_next = neighbours(first, last)
        stack = spread(stat)
        expand_grads[layer] = outer(f"outer_expand_{layer}", k["act_two"], dz_three, "ba", "ha")
        frame, pre_one, stat, sums_two = call(
            f"spatial_back_{layer}", functools.partial(spatial_back_kernel, layer, total, shape, padded), "svvvvvvvvvvvvw",
            (flags, pre_two, grad_prev, grad_next, k["z_two"], *k["z_two_edges"], k["norm_two"], stack, gain_mid, bias_mid, k["z_one"], k["norm_one"], w_spatial),
            [shaped((frame_rows, mid), BF16), mids, pair_mid, pair_mid], [w_two, acc_two, sems_3], 10 * small // 4,
        )
        stack = spread(stat)
        out, places = layout(9, mid, mid, "ha", "ba")
        x = call(
            f"outer_spatial_{layer}", functools.partial(spatial_outer_kernel, places, shape, padded), "vv",
            (frame, k["frame"]), [out],
            [pltpu.VMEM((span + 16, mid), F32), pltpu.VMEM((span, mid), BF16)], 10 * small // 4,
        )[0]
        spatial_grads[layer] = jnp.swapaxes(scatter_sum(x, places, "ha", "ba"), 1, 2)
        if layer == 1:
            b = kept[0]
            dz_one, sums_one, grad, keep, send = call(
                "reduce_back_1", functools.partial(reduce_back_kernel, 1, total), "svvvvvwvvvvvv",
                (flags, pre_one, k["z_one"], k["norm_one"], stack, gain_mid, w_reduce, grad, b["z_three"], b["inputs"], b["norm_three"], gain_out, bias_out),
                [mids_b, pair_mid, outs_f, half_out, half_out],
                [w_one, pltpu.VMEM((pixels, min(BLOCK, chans)), F32), sems], small,
            )
        else:
            dz_one, sums_one = call(
                "reduce_back_0", functools.partial(input_kernel, 0, total), "vvvvv",
                (pre_one, k["z_one"], k["norm_one"], stack, gain_mid), [mids_b, pair_mid],
            )
        reduce_grads[layer] = outer(f"outer_reduce_{layer}", k["inputs"], dz_one, "ha", "ba")
        mid_sums[layer] = jnp.stack([sums_one, sums_two])
    input_grad = call(
        "input_grad", functools.partial(input_grad_kernel, 0), "vvw", (dz_one, grad, w_reduce),
        [outs_f], [w_one, sems], small,
    )[0]
    mid_sums, out_sums = jnp.stack(mid_sums), jnp.stack(out_sums)
    grad_spatial = jnp.stack(spatial_grads)
    return (
        activations.reshape(images.shape),
        input_grad.reshape(images.shape),
        jnp.stack(reduce_grads),
        grad_spatial.reshape((2, 3, 3) + grad_spatial.shape[2:]),
        jnp.stack(expand_grads),
        mid_sums[:, :, 1],
        mid_sums[:, :, 0],
        out_sums[:, 1],
        out_sums[:, 0],
        grad_heads,
    )


def solution(mesh):
    pixels = P("ba", "ha", None, None)
    return jax.shard_map(
        body,
        mesh=mesh,
        in_specs=(pixels, P(), P(), P(), P(), P(), P(), P(), P(), pixels, P("ba", "ha", None)),
        out_specs=(
            pixels,
            pixels,
            P(None, "ha", "ba"),
            P(None, None, None, "ba", "ha"),
            P(None, "ba", "ha"),
            P(),
            P(),
            P(),
            P(),
            P("ha", "ba"),
        ),
        check_vma=False,
    )
```

```python
import functools
import math

import jax
import jax.numpy as jnp
from jax import lax
from jax.experimental import pallas as pl
from jax.experimental.pallas import tpu as pltpu
from jax.sharding import PartitionSpec as P

EPS = 1e-05
SIGN_WIDTH = 0.1
TEMPER = 0.1
ABS_EPS = 0.01
F32, BF16 = jnp.float32, jnp.bfloat16
BOTH = ("ha", "ba")
STEP = 16
BLOCK = 512
VMEM_LIMIT = 60 * 1024 * 1024


def phi(x):
    return 0.5 + 0.5 * lax.erf(x * math.sqrt(0.5))


def gelu(x):
    return x * phi(x)


def gelu_slope(x):
    return phi(x) + x * (1.0 / math.sqrt(2.0 * math.pi)) * jnp.exp(-0.5 * x * x)


def sigmoid(x):
    return 0.5 + 0.5 * jnp.tanh(0.5 * x)


def dot(a, b):
    return jnp.dot(a, b, preferred_element_type=F32)


def dot_nt(a, b):
    return lax.dot_general(a, b, (((1,), (1,)), ((), ())), preferred_element_type=F32)


def dot_tn(a, b):
    return lax.dot_general(a, b, (((0,), (0,)), ((), ())), preferred_element_type=F32)


def row_loop(count, body, init):
    def step(i, carry):
        return body(pl.ds(pl.multiple_of(i * STEP, STEP), STEP), carry)

    return lax.fori_loop(0, count // STEP, step, init)


def fold(x):
    return jnp.sum(x, 0, keepdims=True)


def moments(ref, columns):
    count = ref.shape[0]
    zero = jnp.zeros((STEP, columns.stop - columns.start), F32)
    total = row_loop(count, lambda rows, acc: acc + ref[rows, columns], zero)
    mean = fold(total) * (1.0 / count)

    def centred(rows, acc):
        off = ref[rows, columns] - mean
        return acc + off * off

    return mean, fold(row_loop(count, centred, zero)) * (1.0 / count)


def merged_moments(stack_ref):
    means, squares = stack_ref[:, 0, :], stack_ref[:, 1, :]
    share = 1.0 / means.shape[0]
    mean = fold(means) * share
    off = means - mean
    return mean, lax.rsqrt(fold(squares) * share + fold(off * off) * share + EPS)


def put_halves(core, pair, kept_ref, sent_ref):
    half = pair.shape[1] // 2
    low, high = pair[:, :half], pair[:, half:]
    kept_ref[...] = jnp.where(core == 0, low, high)
    sent_ref[...] = jnp.where(core == 0, high, low)


def take_halves(core, own_ref, other_ref):
    own, other = own_ref[...], other_ref[...]
    return jnp.concatenate([jnp.where(core == 0, own, other), jnp.where(core == 0, other, own)], 1)


def blocks(width, unit=1):
    size = min(max(BLOCK // unit, 1) * unit, width)
    return [slice(i, i + size) for i in range(0, width, size)]


class Stream:
    def __init__(self, src, dst, cuts, sems, rows=False):
        self.copies = []
        for i, c in enumerate(cuts):
            where = (c, slice(None)) if rows else (slice(None), c)
            self.copies.append(pltpu.make_async_copy(src.at[where], dst.at[where], sems.at[i]))

    def start(self, i):
        self.copies[i].start()

    def wait(self, i):
        self.copies[i].wait()


def fetch(streams):
    for i in range(len(streams[0].copies)):
        for stream in streams:
            stream.start(i)


def arrive(streams, i):
    for stream in streams:
        stream.wait(i)


def edges(ref, first_ref, last_ref, shape, padded, centre=None):
    count, rows, width = shape
    for i in range(count):
        for at, out in ((i * rows * width, first_ref), (((i + 1) * rows - 1) * width, last_ref)):
            value = ref[at : at + width, :]
            value = value if centre is None else value - centre
            zero = jnp.zeros((padded - width, value.shape[1]), F32)
            out[i * padded : (i + 1) * padded, :] = jnp.concatenate([value, zero], 0).astype(BF16)


def finish_stats(ref, stat_ref, first_ref, last_ref, shape, padded):
    mean, square = moments(ref, slice(0, ref.shape[1]))
    stat_ref[0:1, :] = mean
    stat_ref[1:2, :] = square
    edges(ref, first_ref, last_ref, shape, padded, mean)


def reduce_kernel(layer, shape, padded, u_ref, w_ref, z_ref, stat_ref, first_ref, last_ref, u_buf, w_buf, sems):
    cuts = blocks(u_ref.shape[1])
    streams = [Stream(u_ref, u_buf, cuts, sems.at[0]), Stream(w_ref.at[layer], w_buf, cuts, sems.at[1], True)]
    fetch(streams)
    for i, c in enumerate(cuts):
        arrive(streams, i)
        part = dot(u_buf[:, c], w_buf[c, :])
        z_ref[...] = part if i == 0 else z_ref[...] + part
    finish_stats(z_ref, stat_ref, first_ref, last_ref, shape, padded)


def fill_frame(frame_ref, shape, padded, sources, make):
    count, rows, width = shape
    prev, own, after = sources
    units = [(prev, i * padded, i * padded, 0) for i in range(count)]
    units += [(after, i * padded, ((rows + 1) * count + i) * padded, 1) for i in range(count)]
    units += [
        (own, (i * rows + r) * width, ((r + 1) * count + i) * padded, None) for i in range(count) for r in range(rows)
    ]
    lanes = frame_ref.shape[1] // 128

    def step(j, carry):
        columns = pl.ds(pl.multiple_of(j * 128, 128), 128)
        zero = jnp.zeros((padded - width, 128), F32)
        for source, start, target, side in units:
            value = make(source, pl.ds(start, width if side is None else padded), columns, side)[:width]
            frame_ref[pl.ds(target, padded), columns] = jnp.concatenate([value, zero], 0).astype(BF16)
        return carry

    lax.fori_loop(0, lanes, step, 0)


def shifted_sum(acc_ref, shape, padded, shifts, out_ref, finish):
    count, rows, width = shape
    lanes = acc_ref.shape[2] // 128
    for j in range(lanes):
        columns = slice(j * 128, (j + 1) * 128)
        for i in range(count):
            for r in range(rows):
                base = 8 + (r * count + i) * padded
                total = None
                for k, shift in enumerate(shifts):
                    part = acc_ref[k, base + shift : base + shift + width, columns]
                    total = part if total is None else total + part
                start = (i * rows + r) * width
                out_ref[start : start + width, columns] = finish(total, slice(start, start + width), columns)


def put_norm(flags_ref, stack_ref, norm_ref):
    mean, scale = merged_moments(stack_ref)
    norm_ref[0:1, :] = mean
    norm_ref[1:2, :] = scale
    norm_ref[2:3, :] = stack_ref[flags_ref[3], 0:1, :]
    norm_ref[3:4, :] = stack_ref[flags_ref[4], 0:1, :]


def edge_value(source, where, columns, side, norm_ref):
    value = source[where, columns]
    return value if side is None else value.astype(F32) + norm_ref[2 + side : 3 + side, columns]


def taps(w_ref, w_buf, sems):
    copies = [pltpu.make_async_copy(w_ref.at[:, kw], w_buf.at[kw], sems.at[kw]) for kw in range(3)]
    for copy in copies:
        copy.start()
    return copies


def spatial_kernel(
    layer, shape, padded,
    flags_ref, z_ref, prev_ref, next_ref, stack_ref, gain_ref, bias_ref, w_ref,
    frame_ref, out_ref, stat_ref, norm_ref, first_ref, last_ref, w_buf, acc_ref, sems,
):
    count, rows, width = shape
    copies = taps(w_ref.at[layer], w_buf, sems)
    put_norm(flags_ref, stack_ref, norm_ref)

    def make(source, where, columns, side):
        off = edge_value(source, where, columns, side, norm_ref) - norm_ref[0:1, columns]
        value = gelu(off * norm_ref[1:2, columns] * gain_ref[layer, 0:1, columns] + bias_ref[layer, 0:1, columns])
        return value if side is None else value * flags_ref[1 + side].astype(F32)

    fill_frame(frame_ref, shape, padded, (prev_ref, z_ref, next_ref), make)
    span = rows * count * padded
    acc_ref[:, 0:8, :] = jnp.zeros((3, 8, acc_ref.shape[2]), F32)
    acc_ref[:, 8 + span :, :] = jnp.zeros((3, 8, acc_ref.shape[2]), F32)
    for kw in range(3):
        copies[kw].wait()
        for kh in range(3):
            start = kh * count * padded
            part = dot(frame_ref[start : start + span, :], w_buf[kw, kh])
            acc_ref[kw, 8 : 8 + span, :] = part if kh == 0 else acc_ref[kw, 8 : 8 + span, :] + part
    shifted_sum(acc_ref, shape, padded, (-1, 0, 1), out_ref, lambda total, where, columns: total)
    finish_stats(out_ref, stat_ref, first_ref, last_ref, shape, padded)


def expand_kernel(
    layer, flags_ref, z_ref, stack_ref, gain_ref, bias_ref, w_ref,
    act_ref, out_ref, kept_ref, sent_ref, norm_ref, w_buf, out_buf, sems,
):
    cuts = blocks(out_ref.shape[1])
    weights = Stream(w_ref.at[layer], w_buf, cuts, sems.at[0])
    result = Stream(out_buf, out_ref, cuts, sems.at[1])
    fetch([weights])
    put_norm(flags_ref, stack_ref, norm_ref)
    mean, scale = norm_ref[0:1, :], norm_ref[1:2, :]
    gain, bias = gain_ref[layer, 1:2, :], bias_ref[layer, 1:2, :]

    def step(rows, carry):
        act_ref[rows, :] = gelu((z_ref[rows, :] - mean) * scale * gain + bias).astype(BF16)
        return carry

    row_loop(z_ref.shape[0], step, 0)
    stats = []
    for i, c in enumerate(cuts):
        weights.wait(i)
        out_buf[:, c] = dot(act_ref[...], w_buf[:, c])
        result.start(i)
        stats.append(jnp.concatenate(moments(out_buf, c), 0))
    put_halves(flags_ref[0], jnp.concatenate(stats, 1), kept_ref, sent_ref)
    arrive_all(result, cuts)


def arrive_all(stream, cuts):
    for i in range(len(cuts)):
        stream.wait(i)


def out_norm(flags_ref, own_ref, other_ref, norm_ref):
    pair = take_halves(flags_ref[0], own_ref, other_ref)
    norm_ref[0:1, :] = pair[0:1]
    norm_ref[1:2, :] = lax.rsqrt(pair[1:2] + EPS)


def summed(z_ref, u_ref, norm_ref, gain_ref, bias_ref, layer, rows, c):
    hat = (z_ref[rows, c] - norm_ref[0:1, c]) * norm_ref[1:2, c]
    return hat, hat * gain_ref[layer : layer + 1, c] + bias_ref[layer : layer + 1, c] + u_ref[rows, c].astype(F32)


def join_kernel(
    layer, shape, padded, flags_ref, z_ref, u_ref, own_ref, other_ref, gain_ref, bias_ref, w_ref,
    state_ref, out_ref, stat_ref, first_ref, last_ref, norm_ref, w_buf, z_buf, u_buf, state_buf, sems,
):
    cuts = blocks(z_ref.shape[1])
    streams = [
        Stream(z_ref, z_buf, cuts, sems.at[0]),
        Stream(u_ref, u_buf, cuts, sems.at[1]),
        Stream(w_ref.at[layer + 1], w_buf, cuts, sems.at[2], True),
    ]
    result = Stream(state_buf, state_ref, cuts, sems.at[3])
    fetch(streams)
    out_norm(flags_ref, own_ref, other_ref, norm_ref)
    for i, c in enumerate(cuts):
        arrive(streams, i)

        def step(rows, carry, c=c):
            state_buf[rows, c] = gelu(
                summed(z_buf, u_buf, norm_ref, gain_ref, bias_ref, layer, rows, c)[1]
            ).astype(BF16)
            return carry

        row_loop(z_ref.shape[0], step, 0)
        result.start(i)
        part = dot(state_buf[:, c], w_buf[c, :])
        out_ref[...] = part if i == 0 else out_ref[...] + part
    finish_stats(out_ref, stat_ref, first_ref, last_ref, shape, padded)
    arrive_all(result, cuts)


def heads_kernel(
    layer, total, flags_ref, z_ref, u_ref, own_ref, other_ref, gain_ref, bias_ref, w_ref, want_ref, level_ref,
    state_ref, cot_ref, grad_ref, kept_ref, sent_ref, norm_ref,
    w_buf, z_buf, u_buf, want_buf, state_buf, grad_buf, pred_ref, part_ref, sems,
):
    pixels = z_ref.shape[0]
    cuts = blocks(z_ref.shape[1])
    streams = [
        Stream(z_ref, z_buf, cuts, sems.at[0]),
        Stream(u_ref, u_buf, cuts, sems.at[1]),
        Stream(w_ref, w_buf, cuts, sems.at[2], True),
    ]
    result = Stream(state_buf, state_ref, cuts, sems.at[3])
    gradient = Stream(grad_buf, grad_ref, cuts, sems.at[4])
    wanted_copy = pltpu.make_async_copy(want_ref, want_buf, sems.at[5, 0])
    fetch(streams)
    wanted_copy.start()
    out_norm(flags_ref, own_ref, other_ref, norm_ref)
    for i, c in enumerate(cuts):
        arrive(streams, i)

        def step(rows, carry, c=c):
            state_buf[rows, c] = gelu(
                summed(z_buf, u_buf, norm_ref, gain_ref, bias_ref, layer, rows, c)[1]
            ).astype(BF16)
            return carry

        row_loop(pixels, step, 0)
        result.start(i)
        part = dot(state_buf[:, c], w_buf[c, :])
        pred_ref[...] = part if i == 0 else pred_ref[...] + part
    wanted_copy.wait()

    def error(rows, carry):
        wanted = want_buf[rows, :].astype(F32) * 0.25
        cot_ref[rows, :] = ((pred_ref[rows, :] - wanted) * (1.0 / math.sqrt(total))).astype(BF16)
        return carry

    row_loop(pixels, error, 0)
    head = cot_ref.shape[1] // 3
    amplify = math.sqrt(total)
    stats = []
    for i, c in enumerate(cuts):
        for t in range(3):
            columns = slice(t * head, (t + 1) * head)
            part_ref[t] = dot_nt(cot_ref[:, columns], w_buf[c, columns])
        width = (c.stop - c.start) // 2

        def drop(rows, carry, c=c, width=width):
            shift = level_ref[rows, :] * (-0.5 / TEMPER) + 0.25 / TEMPER
            out = []
            for k in range(2):
                local = slice(k * width, (k + 1) * width)
                here = slice(c.start + k * width, c.start + (k + 1) * width)
                scaled = [part_ref[t, rows, local] * amplify for t in range(3)]
                spread = None
                for h in scaled:
                    square = h * h + ABS_EPS
                    root = square * lax.rsqrt(square)
                    spread = root if spread is None else spread + root
                agree = (scaled[0] + scaled[1]) + scaled[2]
                lean = jnp.tanh(agree / spread * (0.25 / TEMPER) + shift)
                sides = None
                for h in scaled:
                    side = h * jnp.tanh(h * (0.5 / SIGN_WIDTH))
                    sides = side if sides is None else sides + side
                merged = (0.5 / amplify) * (agree + lean * sides)
                hat, pre = summed(z_buf, u_buf, norm_ref, gain_ref, bias_ref, layer, rows, here)
                grad = gelu_slope(pre) * merged
                grad_buf[rows, here] = grad
                out.append((carry[k][0] + grad, carry[k][1] + grad * hat))
            return tuple(out)

        zero = jnp.zeros((STEP, width), F32)
        sums = row_loop(pixels, drop, ((zero, zero), (zero, zero)))
        gradient.start(i)
        stats += [jnp.concatenate([fold(s) for s in pair], 0) for pair in sums]
    put_halves(flags_ref[0], jnp.concatenate(stats, 1), kept_ref, sent_ref)
    arrive_all(result, cuts)
    arrive_all(gradient, cuts)


def expand_back_kernel(
    layer, total, shape, padded, flags_ref, grad_ref, z_out_ref, norm_out_ref, own_ref, other_ref, gain_out_ref,
    z_ref, norm_ref, gain_ref, bias_ref, w_ref,
    dz_ref, pre_ref, stat_ref, sums_ref, first_ref, last_ref, w_buf, grad_buf, z_buf, dz_buf, acc_ref, sems,
):
    pixels = z_ref.shape[0]
    cuts = blocks(grad_ref.shape[1])
    streams = [
        Stream(grad_ref, grad_buf, cuts, sems.at[0]),
        Stream(z_out_ref, z_buf, cuts, sems.at[1]),
        Stream(w_ref.at[layer], w_buf, cuts, sems.at[2]),
    ]
    result = Stream(dz_buf, dz_ref, cuts, sems.at[3])
    fetch(streams)
    sums_ref[...] = take_halves(flags_ref[0], own_ref, other_ref)
    for i, c in enumerate(cuts):
        arrive(streams, i)
        mean, scale = norm_out_ref[0:1, c], norm_out_ref[1:2, c]
        d_bias, d_gain = sums_ref[0:1, c] * (1.0 / total), sums_ref[1:2, c] * (1.0 / total)
        factor = gain_out_ref[layer : layer + 1, c] * scale

        def step(rows, carry, c=c, mean=mean, scale=scale, d_bias=d_bias, d_gain=d_gain, factor=factor):
            hat = (z_buf[rows, c] - mean) * scale
            dz_buf[rows, c] = (factor * (grad_buf[rows, c] - d_bias - hat * d_gain)).astype(BF16)
            return carry

        row_loop(pixels, step, 0)
        result.start(i)
        part = dot_nt(dz_buf[:, c], w_buf[:, c])
        acc_ref[...] = part if i == 0 else acc_ref[...] + part
    mean, scale = norm_ref[0:1, :], norm_ref[1:2, :]
    gain, bias = gain_ref[layer, 1:2, :], bias_ref[layer, 1:2, :]

    def slope(rows, carry):
        hat = (z_ref[rows, :] - mean) * scale
        grad = gelu_slope(hat * gain + bias) * acc_ref[rows, :]
        pre_ref[rows, :] = grad
        return carry[0] + grad, carry[1] + grad * hat

    zero = jnp.zeros((STEP, z_ref.shape[1]), F32)
    s_bias, s_gain = row_loop(pixels, slope, (zero, zero))
    stat_ref[0:1, :] = fold(s_bias)
    stat_ref[1:2, :] = fold(s_gain)
    edges(pre_ref, first_ref, last_ref, shape, padded)
    arrive_all(result, cuts)


def spatial_back_kernel(
    layer, total, shape, padded, flags_ref, grad_ref, grad_prev_ref, grad_next_ref, z_ref, z_prev_ref, z_next_ref,
    norm_ref, stack_ref, gain_ref, bias_ref, z_in_ref, norm_in_ref, w_ref,
    frame_ref, pre_ref, stat_ref, sums_ref, w_buf, acc_ref, sems,
):
    count, rows, width = shape
    copies = taps(w_ref.at[layer], w_buf, sems)
    sums_ref[0:1, :] = fold(stack_ref[:, 0, :])
    sums_ref[1:2, :] = fold(stack_ref[:, 1, :])

    def make(source, where, columns, side):
        scale = norm_ref[1:2, columns]
        hat = (edge_value(source[1], where, columns, side, norm_ref) - norm_ref[0:1, columns]) * scale
        d_bias, d_gain = sums_ref[0:1, columns] * (1.0 / total), sums_ref[1:2, columns] * (1.0 / total)
        value = gain_ref[layer, 1:2, columns] * scale * (source[0][where, columns].astype(F32) - d_bias - hat * d_gain)
        return value if side is None else value * flags_ref[1 + side].astype(F32)

    sources = ((grad_prev_ref, z_prev_ref), (grad_ref, z_ref), (grad_next_ref, z_next_ref))
    fill_frame(frame_ref, shape, padded, sources, make)
    span = rows * count * padded
    acc_ref[:, 0:8, :] = jnp.zeros((3, 8, acc_ref.shape[2]), F32)
    acc_ref[:, 8 + span :, :] = jnp.zeros((3, 8, acc_ref.shape[2]), F32)
    for kw in range(3):
        copies[kw].wait()
        for kh in range(3):
            start = (2 - kh) * count * padded
            part = dot_nt(frame_ref[start : start + span, :], w_buf[kw, kh])
            acc_ref[kw, 8 : 8 + span, :] = part if kh == 0 else acc_ref[kw, 8 : 8 + span, :] + part
    lanes = acc_ref.shape[2] // 128
    totals = [[None, None] for _ in range(lanes)]

    def finish(value, where, columns):
        hat = (z_in_ref[where, columns] - norm_in_ref[0:1, columns]) * norm_in_ref[1:2, columns]
        grad = gelu_slope(hat * gain_ref[layer, 0:1, columns] + bias_ref[layer, 0:1, columns]) * value
        keep = totals[columns.start // 128]
        for k, term in enumerate((grad, grad * hat)):
            keep[k] = fold(term) if keep[k] is None else keep[k] + fold(term)
        return grad

    shifted_sum(acc_ref, shape, padded, (1, 0, -1), pre_ref, finish)
    for j in range(lanes):
        for k in range(2):
            stat_ref[k : k + 1, j * 128 : (j + 1) * 128] = totals[j][k]


def reduce_back_start(layer, total, grad_ref, z_ref, norm_ref, stack_ref, gain_ref, dz_ref, sums_ref):
    sums_ref[0:1, :] = fold(stack_ref[:, 0, :])
    sums_ref[1:2, :] = fold(stack_ref[:, 1, :])
    mean, scale = norm_ref[0:1, :], norm_ref[1:2, :]
    d_bias, d_gain = sums_ref[0:1, :] * (1.0 / total), sums_ref[1:2, :] * (1.0 / total)
    factor = gain_ref[layer, 0:1, :] * scale

    def step(rows, carry):
        hat = (z_ref[rows, :] - mean) * scale
        dz_ref[rows, :] = (factor * (grad_ref[rows, :] - d_bias - hat * d_gain)).astype(BF16)
        return carry

    row_loop(z_ref.shape[0], step, 0)


def reduce_back_kernel(
    layer, total, flags_ref, grad_ref, z_ref, norm_ref, stack_ref, gain_ref, w_ref, out_grad_ref,
    z_out_ref, u_ref, norm_out_ref, gain_out_ref, bias_out_ref,
    dz_ref, sums_ref, next_ref, kept_ref, sent_ref, w_buf, grad_buf, z_buf, u_buf, next_buf, part_ref, sems,
):
    cuts = blocks(out_grad_ref.shape[1])
    streams = [
        Stream(w_ref.at[layer], w_buf, cuts, sems.at[0], True),
        Stream(out_grad_ref, grad_buf, cuts, sems.at[1]),
        Stream(z_out_ref, z_buf, cuts, sems.at[2]),
        Stream(u_ref, u_buf, cuts, sems.at[3]),
    ]
    result = Stream(next_buf, next_ref, cuts, sems.at[4])
    fetch(streams)
    reduce_back_start(layer, total, grad_ref, z_ref, norm_ref, stack_ref, gain_ref, dz_ref, sums_ref)
    stats = []
    for i, c in enumerate(cuts):
        arrive(streams, i)
        part_ref[...] = dot_nt(dz_ref[...], w_buf[c, :])

        def slope(rows, carry, c=c):
            hat, pre = summed(z_buf, u_buf, norm_out_ref, gain_out_ref, bias_out_ref, layer - 1, rows, c)
            grad = gelu_slope(pre) * (grad_buf[rows, c] + part_ref[rows, :])
            next_buf[rows, c] = grad
            return carry[0] + grad, carry[1] + grad * hat

        zero = jnp.zeros((STEP, c.stop - c.start), F32)
        sums = row_loop(z_ref.shape[0], slope, (zero, zero))
        result.start(i)
        stats.append(jnp.concatenate([fold(s) for s in sums], 0))
    put_halves(flags_ref[0], jnp.concatenate(stats, 1), kept_ref, sent_ref)
    arrive_all(result, cuts)


def input_kernel(layer, total, grad_ref, z_ref, norm_ref, stack_ref, gain_ref, dz_ref, sums_ref):
    reduce_back_start(layer, total, grad_ref, z_ref, norm_ref, stack_ref, gain_ref, dz_ref, sums_ref)


def input_grad_kernel(layer, dz_ref, out_grad_ref, w_ref, next_ref, w_buf, grad_buf, next_buf, sems):
    cuts = blocks(out_grad_ref.shape[1])
    streams = [
        Stream(w_ref.at[layer], w_buf, cuts, sems.at[0], True),
        Stream(out_grad_ref, grad_buf, cuts, sems.at[1]),
    ]
    result = Stream(next_buf, next_ref, cuts, sems.at[2])
    fetch(streams)
    for i, c in enumerate(cuts):
        arrive(streams, i)
        next_buf[:, c] = grad_buf[:, c] + dot_nt(dz_ref[...], w_buf[c, :])
        result.start(i)
    arrive_all(result, cuts)


def store_halves(core, value_ref, axis, size, store):
    for which, bit in ((0, core), (1, 1 - core)):
        for x in range(value_ref.shape[axis] // (2 * size)):
            piece = pl.ds(pl.multiple_of((2 * x + bit) * size, 128), size)
            store(which, x, value_ref[piece, :] if axis == 0 else value_ref[:, piece])


def place(index):
    return index & 1, (index >> 1) & 1, index >> 2


def expand_outer_kernel(flags_ref, left_ref, right_ref, kept_ref, sent_ref, value_ref):
    outs = (kept_ref, sent_ref)
    for c in blocks(right_ref.shape[1]):
        value_ref[...] = dot_tn(left_ref[...], right_ref[:, c])

        def store(which, x, piece, c=c):
            piece = piece.astype(BF16)
            for at in range(0, piece.shape[1], 256):
                y, low, high = place((c.start + at) // 256)
                for half in range(2):
                    outs[which][x, y, low, high, half * 128 : (half + 1) * 128, :] = piece[
                        :, at + half * 128 : at + (half + 1) * 128
                    ]

        store_halves(flags_ref[0], value_ref, 0, 128, store)


def reduce_outer_kernel(flags_ref, left_ref, right_ref, kept_ref, sent_ref, value_ref):
    outs = (kept_ref, sent_ref)
    for c in blocks(left_ref.shape[1]):
        value_ref[...] = dot_tn(left_ref[:, c], right_ref[...])

        def store(which, x, piece, c=c):
            piece = piece.astype(BF16)
            for at in range(0, piece.shape[0], 256):
                outs[which][(x, *place((c.start + at) // 256))] = piece[at : at + 256, :]

        store_halves(flags_ref[0], value_ref, 1, 128, store)


def spatial_taps(shape, padded, grad_ref, frame_ref, line_ref, moved_ref, tap):
    count, rows, width = shape
    span = rows * count * padded
    start = count * padded
    line_ref[0:8, :] = jnp.zeros((8, line_ref.shape[1]), F32)
    line_ref[8 + span :, :] = jnp.zeros((8, line_ref.shape[1]), F32)
    line_ref[8 : 8 + span, :] = grad_ref[start : start + span, :].astype(F32)
    for kw in range(3):
        for b in range(0, span, padded):
            for c in range(0, line_ref.shape[1], 128):
                moved_ref[b : b + padded, c : c + 128] = line_ref[
                    8 + b + 1 - kw : 8 + b + 1 - kw + padded, c : c + 128
                ].astype(BF16)
        for kh in range(3):
            at = kh * count * padded
            tap(3 * kh + kw, dot_tn(moved_ref[...], frame_ref[at : at + span, :]))


def spatial_outer_kernel(
    shape, padded, flags_ref, grad_ref, frame_ref, kept_ref, sent_ref, line_ref, moved_ref, value_ref
):
    outs = (kept_ref, sent_ref)

    def tap(k, value):
        value_ref[...] = value

        def store(which, x, piece):
            piece = piece.astype(BF16)
            for at in range(0, piece.shape[0], 64):
                outs[which][(x, *place(at // 64), slice(k * 64, (k + 1) * 64))] = piece[at : at + 64, :]

        store_halves(flags_ref[0], value_ref, 1, 128, store)

    spatial_taps(shape, padded, grad_ref, frame_ref, line_ref, moved_ref, tap)


def spatial_plain_kernel(shape, padded, grad_ref, frame_ref, out_ref, line_ref, moved_ref):
    def tap(k, value):
        out_ref[k] = value.astype(BF16)

    spatial_taps(shape, padded, grad_ref, frame_ref, line_ref, moved_ref, tap)


def early_outer_kernel(cot_ref, state_ref, act_ref, dz_ref, out_ref, part_ref, sem):
    first = 0
    for left_ref, right_ref in ((cot_ref, state_ref), (act_ref, dz_ref)):
        height = left_ref.shape[1] // out_ref.shape[1]
        for a in blocks(left_ref.shape[1], height):
            for b in blocks(right_ref.shape[1]):
                value = dot_tn(left_ref[:, a], right_ref[:, b]).astype(BF16)
                for i in range(0, value.shape[0], height):
                    for j in range(0, value.shape[1], 128):
                        at = first + ((b.start + j) // 128 % 2) * height
                        part_ref[(b.start + j) // 256, (a.start + i) // height, at : at + height, :] = value[
                            i : i + height, j : j + 128
                        ]
        first += 2 * height
    copy = pltpu.make_async_copy(part_ref, out_ref.at[:, :, 0:first, :], sem.at[0])
    copy.start()
    copy.wait()


def early_spatial_kernel(
    shape, padded, grad_ref, frame_ref, held_ref, out_ref, line_ref, moved_ref, part_ref, sem
):
    def tap(k, value):
        for j in range(part_ref.shape[1]):
            columns = value[:, j * 128 : (j + 1) * 128].astype(BF16)
            for i in range(part_ref.shape[0]):
                part_ref[i, j, k * 64 : (k + 1) * 64, :] = columns[i * 64 : (i + 1) * 64, :]

    spatial_taps(shape, padded, grad_ref, frame_ref, line_ref, moved_ref, tap)
    rows = part_ref.shape[2]
    copy = pltpu.make_async_copy(part_ref, out_ref.at[:, :, out_ref.shape[2] - rows :, :], sem.at[0])
    copy.start()
    copy.wait()


def add_split_kernel(splits, flags_ref, *refs):
    refs = list(refs)
    outs = refs[-2 * len(splits) :]
    for n, (sources, flag, axis) in enumerate(splits):
        offset = 0
        for kept, got, first, rows in sources:
            lead = refs[kept].shape[:-2]
            others = [d for d in lead[:axis] + lead[axis + 1 :]]
            spots = [()]
            for d in others:
                spots = [spot + (i,) for spot in spots for i in range(d)]
            for which in range(2):
                index = flags_ref[flag] if which == 0 else 1 - flags_ref[flag]
                for spot in spots:
                    where = spot[:axis] + (index,) + spot[axis:] + (slice(first, first + rows), slice(None))
                    value = refs[kept][where].astype(F32) + refs[got][where].astype(F32)
                    outs[2 * n + which][spot + (slice(offset, offset + rows), slice(None))] = value.astype(BF16)
            offset += rows


def shaped(shape, dtype=F32):
    return jax.ShapeDtypeStruct(shape, dtype)


KINDS = {
    "v": pl.BlockSpec(memory_space=pltpu.VMEM),
    "h": pl.BlockSpec(memory_space=pltpu.HBM),
    "s": pl.BlockSpec(memory_space=pltpu.SMEM),
}


def call(name, kernel, specs, args, out_specs, outs, scratch=(), sems=None, flops=0, aliases=None):
    nbytes = sum(math.prod(o.shape) * o.dtype.itemsize for o in outs)
    return pl.pallas_call(
        kernel,
        out_shape=outs,
        in_specs=[KINDS[s] for s in specs],
        out_specs=[KINDS[s] for s in out_specs],
        scratch_shapes=[pltpu.VMEM(s.shape, s.dtype) for s in scratch]
        + ([] if sems is None else [pltpu.SemaphoreType.DMA(sems)]),
        compiler_params=pltpu.CompilerParams(vmem_limit_bytes=VMEM_LIMIT),
        cost_estimate=pl.CostEstimate(flops=flops, bytes_accessed=2 * nbytes, transcendentals=0),
        input_output_aliases=aliases or {},
        name=name,
    )(*args)


def spread(x, groups=None, count=None):
    count = count or lax.axis_size(BOTH)
    copies = jnp.broadcast_to(x[None], (count,) + x.shape)
    return lax.all_to_all(copies, BOTH, 0, 0, tiled=True, axis_index_groups=groups)


def merge_moments(stack):
    means, squares = stack[:, 0], stack[:, 1]
    mean = jnp.mean(means, 0)
    off = means - mean
    return jnp.stack([mean, jnp.mean(squares, 0) + jnp.mean(off * off, 0)])


def merge_sums(stack):
    return jnp.sum(stack, 0)


def share_halves(kept, sent, merge):
    devices, cores = lax.axis_size(BOTH), lax.axis_size("ba")
    swap = [(i, i ^ 1) for i in range(cores)]
    pair = merge(jnp.stack([kept, lax.ppermute(sent, "ba", swap)]))
    groups = [list(range(c, devices, 2)) for c in range(2)]
    own = merge(spread(pair, groups, devices // 2))
    return own, lax.ppermute(own, "ba", swap)


def neighbours(first, last):
    devices = lax.axis_size("ha")
    up = [(i, i + 1) for i in range(devices - 1)]
    down = [(j, i) for i, j in up]
    return lax.ppermute(last, "ha", up), lax.ppermute(first, "ha", down)


def swap(x, axis, bit):
    return lax.ppermute(x, axis, [(i, i ^ bit) for i in range(lax.axis_size(axis))])


CORE, LOW_X, Y, LOW_Z, HIGH_Z = 0, 5, 6, 7, 8


def add_split(name, flags, arrays, splits):
    outs = []
    for sources, _, axis in splits:
        lead = arrays[sources[0][0]].shape[:-2]
        shape = lead[:axis] + lead[axis + 1 :] + (sum(rows for *_, rows in sources), 128)
        outs += [shaped(shape, BF16)] * 2
    return call(
        name, functools.partial(add_split_kernel, splits), "s" + "v" * len(arrays), [flags, *arrays],
        "v" * len(outs), outs,
    )


class Moving:
    def __init__(self, name, flags, pairs):
        self.name, self.flags = name, flags
        self.rows = [kept.shape[-2] for kept, _ in pairs]
        self.kept = [kept for kept, _ in pairs]
        self.got = [swap(sent, "ba", 1) for _, sent in pairs]
        self.stage = 0

    def state(self):
        return self.kept

    def put(self, state):
        self.kept = state

    def advance(self):
        arrays = []
        for kept, got in zip(self.kept, self.got):
            arrays += [kept, got]
        name = f"sum_{self.name}_{self.stage}"
        if self.stage == 0:
            halves = [rows // 2 for rows in self.rows]
            splits = [
                ([(2 * i, 2 * i + 1, 0, half) for i, half in enumerate(halves)], LOW_X, 0),
                ([(2 * i, 2 * i + 1, half, half) for i, half in enumerate(halves)], Y, 1),
            ]
        elif self.stage == 1:
            rows = [x.shape[-2] for x in self.kept]
            splits = [([(0, 1, 0, rows[0])], Y, 0), ([(2, 3, 0, rows[1])], LOW_X, 0)]
        elif self.stage == 2:
            splits = [([(2 * i, 2 * i + 1, 0, x.shape[-2]) for i, x in enumerate(self.kept)], LOW_Z, 0)]
        else:
            splits = [([(0, 1, 0, self.kept[0].shape[-2])], HIGH_Z, 0)]
        outs = add_split(name, self.flags, arrays, splits)
        moves = [[("ba", 2), ("ha", 1)], [("ha", 1), ("ba", 2)], [("ha", 2)], [("ha", 4)]][self.stage]
        self.kept = list(outs[0::2])
        self.got = [swap(x, *move) for x, move in zip(outs[1::2], moves)]
        self.stage += 1

    def result(self):
        total = self.kept[0].astype(F32) + self.got[0].astype(F32)
        halves = [rows // 2 for rows in self.rows]
        parts, at = [], 0
        for half in halves + halves:
            parts.append(total[at : at + half])
            at += half
        return list(zip(parts[: len(halves)], parts[len(halves) :]))


def tie(along, moving):
    along, states = lax.optimization_barrier((along, [one.state() for one in moving]))
    for one, state in zip(moving, states):
        one.put(state)
    return along


def scatter_plain(x, row_axis, column_axis):
    for axis in ("ha", "ba"):
        x = lax.psum_scatter(x, axis, scatter_dimension=1 if axis == row_axis else 2, tiled=True)
    return x.astype(F32)


def body(
    images, w_reduce, w_spatial, w_expand, gain_mid, bias_mid, gain_out, bias_out, w_heads, targets, thresholds
):
    count, rows, width, chans = images.shape
    shape = (count, rows, width)
    padded = (width // 16 + 1) * 16
    pixels = count * rows * width
    total = pixels * lax.axis_size(BOTH)
    mid = w_reduce.shape[2]
    head_columns = w_heads.shape[1]
    frame_rows, span = (rows + 2) * count * padded, rows * count * padded
    edge = shaped((count * padded, mid), BF16)
    here, last_row, across = lax.axis_index("ha"), lax.axis_size("ha") - 1, lax.axis_size("ba")
    column = lax.axis_index("ba")
    flags = jnp.stack(
        [
            column % 2, here > 0, here < last_row,
            jnp.maximum(here - 1, 0) * across + column, jnp.minimum(here + 1, last_row) * across + column,
            column // 2 % 2, here % 2, here // 2 % 2, here // 4 % 2,
        ]
    ).astype(jnp.int32)
    cuts = len(blocks(chans))
    pair_mid, norm_mid, pair_out = shaped((2, mid)), shaped((4, mid)), shaped((2, chans))
    half_out = shaped((2, chans // 2))
    mids, outs_f = shaped((pixels, mid)), shaped((pixels, chans))
    mids_b, outs_b = shaped((pixels, mid), BF16), shaped((pixels, chans), BF16)
    w_one, w_three, w_two = shaped((chans, mid), BF16), shaped((mid, chans), BF16), shaped((3, 3, mid, mid), BF16)
    acc_two = shaped((3, span + 16, mid))
    block = shaped((pixels, min(BLOCK, chans)))
    small = 2 * pixels * chans * mid

    state = images.reshape(pixels, chans)
    kept = []
    z_one, stat, first, last = call(
        "reduce_0", functools.partial(reduce_kernel, 0, shape, padded), "hh", (state, w_reduce),
        "vvvv", [mids, pair_mid, edge, edge], [outs_b, w_one], (2, cuts), small,
    )
    for layer in range(2):
        prev, after = neighbours(first, last)
        stack = spread(stat)
        frame, z_two, stat, norm_one, *z_two_edges = call(
            f"spatial_{layer}", functools.partial(spatial_kernel, layer, shape, padded), "svvvvvvh",
            (flags, z_one, prev, after, stack, gain_mid, bias_mid, w_spatial),
            "vvvvvv", [shaped((frame_rows, mid), BF16), mids, pair_mid, norm_mid, edge, edge],
            [w_two, acc_two], (3,), 10 * small // 4,
        )
        stack = spread(stat)
        act_two, z_three, keep, send, norm_two = call(
            f"expand_{layer}", functools.partial(expand_kernel, layer), "svvvvh",
            (flags, z_two, stack, gain_mid, bias_mid, w_expand),
            "vhvvv", [mids_b, outs_f, half_out, half_out, norm_mid], [w_three, outs_f], (2, cuts), small,
        )
        own, other = share_halves(keep, send, merge_moments)
        saved = dict(
            inputs=state, z_one=z_one, norm_one=norm_one, frame=frame, z_two=z_two, z_two_edges=z_two_edges,
            norm_two=norm_two, act_two=act_two, z_three=z_three,
        )
        kept.append(saved)
        if layer == 0:
            state, z_one, stat, first, last, saved["norm_three"] = call(
                "join", functools.partial(join_kernel, 0, shape, padded), "shhvvvvh",
                (flags, z_three, state, own, other, gain_out, bias_out, w_reduce),
                "hvvvvv", [outs_b, mids, pair_mid, edge, edge, pair_out],
                [w_one, outs_f, outs_b, outs_b], (4, cuts), small,
            )
    (own, other), edge_rows = lax.optimization_barrier(((own, other), [k["z_two_edges"] for k in kept]))
    for k, pair in zip(kept, edge_rows):
        k["z_two_edges"] = neighbours(*pair)
    wanted = targets.reshape(pixels, head_columns)
    level = thresholds.reshape(pixels, 1).astype(F32) * 0.001
    heads_wide = shaped((pixels, head_columns))
    state, cot, grad, keep, send, kept[1]["norm_three"] = call(
        "heads", functools.partial(heads_kernel, 1, total), "shhvvvvhhv",
        (flags, z_three, state, own, other, gain_out, bias_out, w_heads, wanted, level),
        "hvhvvv", [outs_b, shaped((pixels, head_columns), BF16), outs_f, half_out, half_out, pair_out],
        [
            shaped((chans, head_columns), BF16), outs_f, outs_b, shaped((pixels, head_columns), jnp.int32),
            outs_b, outs_f, heads_wide, shaped((3,) + block.shape),
        ],
        (6, cuts), 3 * small,
    )
    (keep, send), edge_rows = lax.optimization_barrier(((keep, send), [k["z_two_edges"] for k in kept]))
    for k, pair in zip(kept, edge_rows):
        k["z_two_edges"] = pair
    activations = state
    fast = across == 4 and last_row == 7 and mid == 512 and chans == 2048 and head_columns % 64 == 0
    parts_out = lambda rows: [shaped((2, 2, 2, 2, rows, 128), BF16)] * 2
    square = shaped((mid, mid))

    moving = []
    reduce_grads, spatial_grads, expand_grads = [None, None], [None, None], [None, None]
    mid_sums, out_sums = [None, None], [None, None]
    for layer in (1, 0):
        k = kept[layer]
        own, other = share_halves(keep, send, merge_sums)
        dz_three, pre_two, stat, out_sums[layer], first, last = call(
            f"expand_back_{layer}", functools.partial(expand_back_kernel, layer, total, shape, padded), "shhvvvvvvvvh",
            (flags, grad, k["z_three"], k["norm_three"], own, other, gain_out, k["z_two"], k["norm_two"], gain_mid, bias_mid, w_expand),
            "hvvvvv", [outs_b, mids, pair_mid, pair_out, edge, edge],
            [w_three, outs_f, outs_f, outs_b, mids], (4, cuts), small,
        )
        grad_prev, grad_next = neighbours(first, last)
        stack = spread(stat)
        if not fast:
            expand_grads[layer] = scatter_plain(dot_tn(k["act_two"], dz_three).astype(BF16)[None], "ba", "ha")[0]
            if layer == 1:
                grad_heads = scatter_plain(dot_tn(cot, activations).astype(BF16)[None], "ba", "ha")[0].T
        elif layer == 1:
            rows_early = (2 * head_columns + 2 * mid) // across
            rows_all = rows_early + 9 * mid // (last_row + 1)
            early = call(
                "outer_early", early_outer_kernel, "vvvv", (cot, activations, k["act_two"], dz_three), "h",
                [shaped((last_row + 1, across, rows_all, 128), BF16)],
                [shaped((last_row + 1, across, rows_early, 128), BF16)], (1,), 3 * small,
            )[0]
            stack, early = lax.optimization_barrier((stack, early))
        else:
            expand_pair = call(
                "outer_expand", expand_outer_kernel, "svv", (flags, k["act_two"], dz_three), "vv", parts_out(256),
                [square], flops=small,
            )
            moving.append(Moving("middle", flags, [reduce_pair, expand_pair]))
            moving[0].advance()
            stack = tie(stack, moving)
        frame, pre_one, stat, sums_two = call(
            f"spatial_back_{layer}", functools.partial(spatial_back_kernel, layer, total, shape, padded), "svvvvvvvvvvvvh",
            (flags, pre_two, grad_prev, grad_next, k["z_two"], *k["z_two_edges"], k["norm_two"], stack, gain_mid, bias_mid, k["z_one"], k["norm_one"], w_spatial),
            "vvvv", [shaped((frame_rows, mid), BF16), mids, pair_mid, pair_mid], [w_two, acc_two], (3,), 10 * small // 4,
        )
        stack = spread(stat)
        line, moved = shaped((span + 16, mid)), shaped((span, mid), BF16)
        if fast and layer == 1:
            early = call(
                "outer_spatial_1", functools.partial(early_spatial_kernel, shape, padded), "vvh",
                (frame, k["frame"], early), "h", [shaped(early.shape, BF16)],
                [line, moved, shaped((last_row + 1, across, 9 * mid // (last_row + 1), 128), BF16)], (1,),
                10 * small // 4, {2: 0},
            )[0]
            stack, early = lax.optimization_barrier((stack, early))
            early = early.reshape((-1,) + early.shape[2:])
            early = lax.psum_scatter(early, BOTH, scatter_dimension=0, tiled=True)[0].astype(F32)
            cut = [head_columns // across, 2 * head_columns // across, (2 * head_columns + mid) // across, rows_early]
            early = jnp.split(early, cut)
            grad_heads = jnp.concatenate(early[:2], 1).T
            expand_grads[1] = jnp.concatenate(early[2:4], 1)
            spatial_grads[1] = early[4].reshape(9, mid // (last_row + 1), 128)
        elif fast:
            spatial_pair = call(
                f"outer_spatial_{layer}", functools.partial(spatial_outer_kernel, shape, padded), "svv",
                (flags, frame, k["frame"]), "vv", parts_out(9 * 64), [line, moved, square], flops=10 * small // 4,
            )
        else:
            x = call(
                f"outer_spatial_{layer}", functools.partial(spatial_plain_kernel, shape, padded), "vv",
                (frame, k["frame"]), "v", [shaped((9, mid, mid), BF16)], [line, moved], flops=10 * small // 4,
            )[0]
            spatial_grads[layer] = scatter_plain(x, "ha", "ba")
        if layer == 1:
            b = kept[0]
            dz_one, sums_one, grad, keep, send = call(
                "reduce_back_1", functools.partial(reduce_back_kernel, 1, total), "svvvvvhhhhvvv",
                (flags, pre_one, k["z_one"], k["norm_one"], stack, gain_mid, w_reduce, grad, b["z_three"], b["inputs"], b["norm_three"], gain_out, bias_out),
                "vvhvv", [mids_b, pair_mid, outs_f, half_out, half_out],
                [w_one, outs_f, outs_f, outs_b, outs_f, block], (5, cuts), small,
            )
        else:
            if fast:
                moving.append(Moving("spatial", flags, [spatial_pair]))
                moving[0].advance()
                stack = tie(stack, moving)
            dz_one, sums_one = call(
                "reduce_back_0", functools.partial(input_kernel, 0, total), "vvvvv",
                (pre_one, k["z_one"], k["norm_one"], stack, gain_mid), "vv", [mids_b, pair_mid],
            )
        if fast:
            reduce_pair = call(
                f"outer_reduce_{layer}", reduce_outer_kernel, "svv", (flags, k["inputs"], dz_one), "vv", parts_out(256),
                [square], flops=small,
            )
            if layer == 0:
                moving[1].advance()
                moving.append(Moving("last", flags, [reduce_pair]))
                moving[2].advance()
                dz_one = tie(dz_one, moving)
        else:
            reduce_grads[layer] = scatter_plain(dot_tn(k["inputs"], dz_one).astype(BF16)[None], "ha", "ba")[0]
        mid_sums[layer] = jnp.stack([sums_one, sums_two])
    input_grad = call(
        "input_grad", functools.partial(input_grad_kernel, 0), "vhh", (dz_one, grad, w_reduce),
        "h", [outs_f], [w_one, outs_f, outs_f], (3, cuts), small,
    )[0]
    if fast:
        while moving[-1].stage < 4:
            for one in moving:
                if one.stage < 4:
                    one.advance()
        (reduce_one, expand_none), (spatial_none,), (reduce_none,) = [one.result() for one in moving]
        reduce_grads = [jnp.concatenate(pair) for pair in (reduce_none, reduce_one)]
        spatial_grads[0] = jnp.concatenate(spatial_none).reshape(spatial_grads[1].shape)
        expand_grads[0] = jnp.concatenate(expand_none, 1)
    mid_sums, out_sums = jnp.stack(mid_sums), jnp.stack(out_sums)
    grad_spatial = jnp.swapaxes(jnp.stack(spatial_grads), 2, 3)
    return (
        activations.reshape(images.shape),
        input_grad.reshape(images.shape),
        jnp.stack(reduce_grads),
        grad_spatial.reshape((2, 3, 3) + grad_spatial.shape[2:]),
        jnp.stack(expand_grads),
        mid_sums[:, :, 1],
        mid_sums[:, :, 0],
        out_sums[:, 1],
        out_sums[:, 0],
        grad_heads,
    )


def solution(mesh):
    pixels = P("ba", "ha", None, None)
    return jax.shard_map(
        body,
        mesh=mesh,
        in_specs=(pixels, P(), P(), P(), P(), P(), P(), P(), P(), pixels, P("ba", "ha", None)),
        out_specs=(
            pixels,
            pixels,
            P(None, "ha", "ba"),
            P(None, None, None, "ba", "ha"),
            P(None, "ba", "ha"),
            P(),
            P(),
            P(),
            P(),
            P("ha", "ba"),
        ),
        check_vma=False,
    )
```

```python
import functools
import math

import jax
import jax.numpy as jnp
from jax import lax
from jax.experimental import pallas as pl
from jax.experimental.pallas import tpu as pltpu
from jax.sharding import PartitionSpec as P

EPS = 1e-05
SIGN_WIDTH = 0.1
TEMPER = 0.1
ABS_EPS = 0.01
F32, BF16 = jnp.float32, jnp.bfloat16
BOTH = ("ha", "ba")
STEP = 16
BLOCK = 512
VMEM_LIMIT = 60 * 1024 * 1024
SMALL_LIMIT = 24 * 1024 * 1024


def phi(x):
    return 0.5 + 0.5 * lax.erf(x * math.sqrt(0.5))


def gelu(x):
    return x * phi(x)


def gelu_slope(x):
    return phi(x) + x * (1.0 / math.sqrt(2.0 * math.pi)) * jnp.exp(-0.5 * x * x)


def sigmoid(x):
    return 0.5 + 0.5 * jnp.tanh(0.5 * x)


def dot(a, b):
    return jnp.dot(a, b, preferred_element_type=F32)


def dot_nt(a, b):
    return lax.dot_general(a, b, (((1,), (1,)), ((), ())), preferred_element_type=F32)


def dot_tn(a, b):
    return lax.dot_general(a, b, (((0,), (0,)), ((), ())), preferred_element_type=F32)


def row_loop(count, body, init):
    def step(i, carry):
        return body(pl.ds(pl.multiple_of(i * STEP, STEP), STEP), carry)

    return lax.fori_loop(0, count // STEP, step, init)


def fold(x):
    return jnp.sum(x, 0, keepdims=True)


def moments(ref, columns):
    count = ref.shape[0]
    zero = jnp.zeros((STEP, columns.stop - columns.start), F32)
    total = row_loop(count, lambda rows, acc: acc + ref[rows, columns], zero)
    mean = fold(total) * (1.0 / count)

    def centred(rows, acc):
        off = ref[rows, columns] - mean
        return acc + off * off

    return mean, fold(row_loop(count, centred, zero)) * (1.0 / count)


def merged_moments(stack_ref):
    means, squares = stack_ref[:, 0, :], stack_ref[:, 1, :]
    share = 1.0 / means.shape[0]
    mean = fold(means) * share
    off = means - mean
    return mean, lax.rsqrt(fold(squares) * share + fold(off * off) * share + EPS)


def put_halves(core, pair, kept_ref, sent_ref):
    half = pair.shape[1] // 2
    low, high = pair[:, :half], pair[:, half:]
    kept_ref[...] = jnp.where(core == 0, low, high)
    sent_ref[...] = jnp.where(core == 0, high, low)


def take_halves(core, own_ref, other_ref):
    own, other = own_ref[...], other_ref[...]
    return jnp.concatenate([jnp.where(core == 0, own, other), jnp.where(core == 0, other, own)], 1)


def blocks(width, unit=1):
    size = min(max(BLOCK // unit, 1) * unit, width)
    return [slice(i, i + size) for i in range(0, width, size)]


class Stream:
    def __init__(self, src, dst, cuts, sems, rows=False):
        self.copies = []
        for i, c in enumerate(cuts):
            where = (c, slice(None)) if rows else (slice(None), c)
            self.copies.append(pltpu.make_async_copy(src.at[where], dst.at[where], sems.at[i]))

    def start(self, i):
        self.copies[i].start()

    def wait(self, i):
        self.copies[i].wait()


def fetch(streams):
    for i in range(len(streams[0].copies)):
        for stream in streams:
            stream.start(i)


def arrive(streams, i):
    for stream in streams:
        stream.wait(i)


def edges(ref, first_ref, last_ref, shape, padded, centre=None):
    count, rows, width = shape
    for i in range(count):
        for at, out in ((i * rows * width, first_ref), (((i + 1) * rows - 1) * width, last_ref)):
            value = ref[at : at + width, :]
            value = value if centre is None else value - centre
            zero = jnp.zeros((padded - width, value.shape[1]), F32)
            out[i * padded : (i + 1) * padded, :] = jnp.concatenate([value, zero], 0).astype(BF16)


def put_copies(stat_ref, columns, first, second):
    pair = jnp.concatenate([first, second], 0)
    stat_ref[:, :, columns] = jnp.broadcast_to(pair[None], (stat_ref.shape[0],) + pair.shape)


def finish_stats(ref, stat_ref, first_ref, last_ref, shape, padded):
    mean, square = moments(ref, slice(0, ref.shape[1]))
    put_copies(stat_ref, slice(0, ref.shape[1]), mean, square)
    edges(ref, first_ref, last_ref, shape, padded, mean)


def reduce_kernel(layer, shape, padded, u_ref, w_ref, z_ref, stat_ref, first_ref, last_ref, u_buf, w_buf, sems):
    cuts = blocks(u_ref.shape[1])
    streams = [Stream(u_ref, u_buf, cuts, sems.at[0]), Stream(w_ref.at[layer], w_buf, cuts, sems.at[1], True)]
    fetch(streams)
    for i, c in enumerate(cuts):
        arrive(streams, i)
        part = dot(u_buf[:, c], w_buf[c, :])
        z_ref[...] = part if i == 0 else z_ref[...] + part
    finish_stats(z_ref, stat_ref, first_ref, last_ref, shape, padded)


def fill_frame(frame_ref, shape, padded, sources, make):
    count, rows, width = shape
    prev, own, after = sources
    units = [(prev, i * padded, i * padded, 0) for i in range(count)]
    units += [(after, i * padded, ((rows + 1) * count + i) * padded, 1) for i in range(count)]
    units += [
        (own, (i * rows + r) * width, ((r + 1) * count + i) * padded, None) for i in range(count) for r in range(rows)
    ]
    lanes = frame_ref.shape[1] // 128

    def step(j, carry):
        columns = pl.ds(pl.multiple_of(j * 128, 128), 128)
        zero = jnp.zeros((padded - width, 128), F32)
        for source, start, target, side in units:
            value = make(source, pl.ds(start, width if side is None else padded), columns, side)[:width]
            frame_ref[pl.ds(target, padded), columns] = jnp.concatenate([value, zero], 0).astype(BF16)
        return carry

    lax.fori_loop(0, lanes, step, 0)


def shifted_sum(acc_ref, shape, padded, shifts, out_ref, finish):
    count, rows, width = shape
    lanes = acc_ref.shape[2] // 128
    for j in range(lanes):
        columns = slice(j * 128, (j + 1) * 128)
        for i in range(count):
            for r in range(rows):
                base = 8 + (r * count + i) * padded
                total = None
                for k, shift in enumerate(shifts):
                    part = acc_ref[k, base + shift : base + shift + width, columns]
                    total = part if total is None else total + part
                start = (i * rows + r) * width
                out_ref[start : start + width, columns] = finish(total, slice(start, start + width), columns)


def put_norm(flags_ref, stack_ref, norm_ref):
    mean, scale = merged_moments(stack_ref)
    norm_ref[0:1, :] = mean
    norm_ref[1:2, :] = scale
    norm_ref[2:3, :] = stack_ref[flags_ref[3], 0:1, :]
    norm_ref[3:4, :] = stack_ref[flags_ref[4], 0:1, :]


def edge_value(source, where, columns, side, norm_ref):
    value = source[where, columns]
    return value if side is None else value.astype(F32) + norm_ref[2 + side : 3 + side, columns]


def taps(w_ref, w_buf, sems):
    copies = [pltpu.make_async_copy(w_ref.at[:, kw], w_buf.at[kw], sems.at[kw]) for kw in range(3)]
    for copy in copies:
        copy.start()
    return copies


def spatial_kernel(
    layer, shape, padded,
    flags_ref, z_ref, prev_ref, next_ref, stack_ref, gain_ref, bias_ref, w_ref,
    frame_ref, out_ref, stat_ref, norm_ref, first_ref, last_ref, w_buf, acc_ref, sems,
):
    count, rows, width = shape
    copies = taps(w_ref.at[layer], w_buf, sems)
    put_norm(flags_ref, stack_ref, norm_ref)

    def make(source, where, columns, side):
        off = edge_value(source, where, columns, side, norm_ref) - norm_ref[0:1, columns]
        value = gelu(off * norm_ref[1:2, columns] * gain_ref[layer, 0:1, columns] + bias_ref[layer, 0:1, columns])
        return value if side is None else value * flags_ref[1 + side].astype(F32)

    fill_frame(frame_ref, shape, padded, (prev_ref, z_ref, next_ref), make)
    span = rows * count * padded
    acc_ref[:, 0:8, :] = jnp.zeros((3, 8, acc_ref.shape[2]), F32)
    acc_ref[:, 8 + span :, :] = jnp.zeros((3, 8, acc_ref.shape[2]), F32)
    for kw in range(3):
        copies[kw].wait()
        for kh in range(3):
            start = kh * count * padded
            part = dot(frame_ref[start : start + span, :], w_buf[kw, kh])
            acc_ref[kw, 8 : 8 + span, :] = part if kh == 0 else acc_ref[kw, 8 : 8 + span, :] + part
    shifted_sum(acc_ref, shape, padded, (-1, 0, 1), out_ref, lambda total, where, columns: total)
    finish_stats(out_ref, stat_ref, first_ref, last_ref, shape, padded)


def expand_kernel(
    layer, flags_ref, z_ref, stack_ref, gain_ref, bias_ref, w_ref,
    act_ref, out_ref, kept_ref, sent_ref, norm_ref, w_buf, out_buf, sems,
):
    cuts = blocks(out_ref.shape[1])
    weights = Stream(w_ref.at[layer], w_buf, cuts, sems.at[0])
    result = Stream(out_buf, out_ref, cuts, sems.at[1])
    fetch([weights])
    put_norm(flags_ref, stack_ref, norm_ref)
    mean, scale = norm_ref[0:1, :], norm_ref[1:2, :]
    gain, bias = gain_ref[layer, 1:2, :], bias_ref[layer, 1:2, :]

    def step(rows, carry):
        act_ref[rows, :] = gelu((z_ref[rows, :] - mean) * scale * gain + bias).astype(BF16)
        return carry

    row_loop(z_ref.shape[0], step, 0)
    stats = []
    for i, c in enumerate(cuts):
        weights.wait(i)
        out_buf[:, c] = dot(act_ref[...], w_buf[:, c])
        result.start(i)
        stats.append(jnp.concatenate(moments(out_buf, c), 0))
    put_halves(flags_ref[0], jnp.concatenate(stats, 1), kept_ref, sent_ref)
    arrive_all(result, cuts)


def arrive_all(stream, cuts):
    for i in range(len(cuts)):
        stream.wait(i)


def out_norm(flags_ref, own_ref, other_ref, norm_ref):
    pair = take_halves(flags_ref[0], own_ref, other_ref)
    norm_ref[0:1, :] = pair[0:1]
    norm_ref[1:2, :] = lax.rsqrt(pair[1:2] + EPS)


def summed(z_ref, u_ref, norm_ref, gain_ref, bias_ref, layer, rows, c):
    hat = (z_ref[rows, c] - norm_ref[0:1, c]) * norm_ref[1:2, c]
    return hat, hat * gain_ref[layer : layer + 1, c] + bias_ref[layer : layer + 1, c] + u_ref[rows, c].astype(F32)


def join_kernel(
    layer, shape, padded, flags_ref, z_ref, u_ref, own_ref, other_ref, gain_ref, bias_ref, w_ref,
    state_ref, out_ref, stat_ref, first_ref, last_ref, norm_ref, w_buf, z_buf, u_buf, state_buf, sems,
):
    cuts = blocks(z_ref.shape[1])
    streams = [
        Stream(z_ref, z_buf, cuts, sems.at[0]),
        Stream(u_ref, u_buf, cuts, sems.at[1]),
        Stream(w_ref.at[layer + 1], w_buf, cuts, sems.at[2], True),
    ]
    result = Stream(state_buf, state_ref, cuts, sems.at[3])
    fetch(streams)
    out_norm(flags_ref, own_ref, other_ref, norm_ref)
    for i, c in enumerate(cuts):
        arrive(streams, i)

        def step(rows, carry, c=c):
            state_buf[rows, c] = gelu(
                summed(z_buf, u_buf, norm_ref, gain_ref, bias_ref, layer, rows, c)[1]
            ).astype(BF16)
            return carry

        row_loop(z_ref.shape[0], step, 0)
        result.start(i)
        part = dot(state_buf[:, c], w_buf[c, :])
        out_ref[...] = part if i == 0 else out_ref[...] + part
    finish_stats(out_ref, stat_ref, first_ref, last_ref, shape, padded)
    arrive_all(result, cuts)


def heads_kernel(
    layer, total, flags_ref, z_ref, u_ref, own_ref, other_ref, gain_ref, bias_ref, w_ref, want_ref, level_ref,
    state_ref, cot_ref, grad_ref, kept_ref, sent_ref, norm_ref,
    w_buf, z_buf, u_buf, want_buf, state_buf, grad_buf, pred_ref, part_ref, sems,
):
    pixels = z_ref.shape[0]
    cuts = blocks(z_ref.shape[1])
    streams = [
        Stream(z_ref, z_buf, cuts, sems.at[0]),
        Stream(u_ref, u_buf, cuts, sems.at[1]),
        Stream(w_ref, w_buf, cuts, sems.at[2], True),
    ]
    result = Stream(state_buf, state_ref, cuts, sems.at[3])
    gradient = Stream(grad_buf, grad_ref, cuts, sems.at[4])
    wanted_copy = pltpu.make_async_copy(want_ref, want_buf, sems.at[5, 0])
    fetch(streams)
    wanted_copy.start()
    out_norm(flags_ref, own_ref, other_ref, norm_ref)
    for i, c in enumerate(cuts):
        arrive(streams, i)

        def step(rows, carry, c=c):
            state_buf[rows, c] = gelu(
                summed(z_buf, u_buf, norm_ref, gain_ref, bias_ref, layer, rows, c)[1]
            ).astype(BF16)
            return carry

        row_loop(pixels, step, 0)
        result.start(i)
        part = dot(state_buf[:, c], w_buf[c, :])
        pred_ref[...] = part if i == 0 else pred_ref[...] + part
    wanted_copy.wait()

    def error(rows, carry):
        wanted = want_buf[rows, :].astype(F32) * 0.25
        cot_ref[rows, :] = ((pred_ref[rows, :] - wanted) * (1.0 / math.sqrt(total))).astype(BF16)
        return carry

    row_loop(pixels, error, 0)
    head = cot_ref.shape[1] // 3
    amplify = math.sqrt(total)
    stats = []
    for i, c in enumerate(cuts):
        for t in range(3):
            columns = slice(t * head, (t + 1) * head)
            part_ref[t] = dot_nt(cot_ref[:, columns], w_buf[c, columns])
        width = (c.stop - c.start) // 2

        def drop(rows, carry, c=c, width=width):
            shift = level_ref[rows, :] * (-0.5 / TEMPER) + 0.25 / TEMPER
            out = []
            for k in range(2):
                local = slice(k * width, (k + 1) * width)
                here = slice(c.start + k * width, c.start + (k + 1) * width)
                scaled = [part_ref[t, rows, local] * amplify for t in range(3)]
                spread = None
                for h in scaled:
                    square = h * h + ABS_EPS
                    root = square * lax.rsqrt(square)
                    spread = root if spread is None else spread + root
                agree = (scaled[0] + scaled[1]) + scaled[2]
                lean = jnp.tanh(agree / spread * (0.25 / TEMPER) + shift)
                sides = None
                for h in scaled:
                    side = h * jnp.tanh(h * (0.5 / SIGN_WIDTH))
                    sides = side if sides is None else sides + side
                merged = (0.5 / amplify) * (agree + lean * sides)
                hat, pre = summed(z_buf, u_buf, norm_ref, gain_ref, bias_ref, layer, rows, here)
                grad = gelu_slope(pre) * merged
                grad_buf[rows, here] = grad
                out.append((carry[k][0] + grad, carry[k][1] + grad * hat))
            return tuple(out)

        zero = jnp.zeros((STEP, width), F32)
        sums = row_loop(pixels, drop, ((zero, zero), (zero, zero)))
        gradient.start(i)
        stats += [jnp.concatenate([fold(s) for s in pair], 0) for pair in sums]
    put_halves(flags_ref[0], jnp.concatenate(stats, 1), kept_ref, sent_ref)
    arrive_all(result, cuts)
    arrive_all(gradient, cuts)


def expand_back_kernel(
    layer, total, shape, padded, flags_ref, grad_ref, z_out_ref, norm_out_ref, own_ref, other_ref, gain_out_ref,
    z_ref, norm_ref, gain_ref, bias_ref, w_ref,
    dz_ref, pre_ref, stat_ref, sums_ref, first_ref, last_ref, w_buf, grad_buf, z_buf, dz_buf, acc_ref, sems,
):
    pixels = z_ref.shape[0]
    cuts = blocks(grad_ref.shape[1])
    streams = [
        Stream(grad_ref, grad_buf, cuts, sems.at[0]),
        Stream(z_out_ref, z_buf, cuts, sems.at[1]),
        Stream(w_ref.at[layer], w_buf, cuts, sems.at[2]),
    ]
    result = Stream(dz_buf, dz_ref, cuts, sems.at[3])
    fetch(streams)
    sums_ref[...] = take_halves(flags_ref[0], own_ref, other_ref)
    for i, c in enumerate(cuts):
        arrive(streams, i)
        mean, scale = norm_out_ref[0:1, c], norm_out_ref[1:2, c]
        d_bias, d_gain = sums_ref[0:1, c] * (1.0 / total), sums_ref[1:2, c] * (1.0 / total)
        factor = gain_out_ref[layer : layer + 1, c] * scale

        def step(rows, carry, c=c, mean=mean, scale=scale, d_bias=d_bias, d_gain=d_gain, factor=factor):
            hat = (z_buf[rows, c] - mean) * scale
            dz_buf[rows, c] = (factor * (grad_buf[rows, c] - d_bias - hat * d_gain)).astype(BF16)
            return carry

        row_loop(pixels, step, 0)
        result.start(i)
        part = dot_nt(dz_buf[:, c], w_buf[:, c])
        acc_ref[...] = part if i == 0 else acc_ref[...] + part
    mean, scale = norm_ref[0:1, :], norm_ref[1:2, :]
    gain, bias = gain_ref[layer, 1:2, :], bias_ref[layer, 1:2, :]

    def slope(rows, carry):
        hat = (z_ref[rows, :] - mean) * scale
        grad = gelu_slope(hat * gain + bias) * acc_ref[rows, :]
        pre_ref[rows, :] = grad
        return carry[0] + grad, carry[1] + grad * hat

    zero = jnp.zeros((STEP, z_ref.shape[1]), F32)
    s_bias, s_gain = row_loop(pixels, slope, (zero, zero))
    put_copies(stat_ref, slice(0, z_ref.shape[1]), fold(s_bias), fold(s_gain))
    edges(pre_ref, first_ref, last_ref, shape, padded)
    arrive_all(result, cuts)


def spatial_back_kernel(
    layer, total, shape, padded, flags_ref, grad_ref, grad_prev_ref, grad_next_ref, z_ref, z_prev_ref, z_next_ref,
    norm_ref, stack_ref, gain_ref, bias_ref, z_in_ref, norm_in_ref, w_ref,
    frame_ref, pre_ref, stat_ref, sums_ref, w_buf, acc_ref, sems,
):
    count, rows, width = shape
    copies = taps(w_ref.at[layer], w_buf, sems)
    sums_ref[0:1, :] = fold(stack_ref[:, 0, :])
    sums_ref[1:2, :] = fold(stack_ref[:, 1, :])

    def make(source, where, columns, side):
        scale = norm_ref[1:2, columns]
        hat = (edge_value(source[1], where, columns, side, norm_ref) - norm_ref[0:1, columns]) * scale
        d_bias, d_gain = sums_ref[0:1, columns] * (1.0 / total), sums_ref[1:2, columns] * (1.0 / total)
        value = gain_ref[layer, 1:2, columns] * scale * (source[0][where, columns].astype(F32) - d_bias - hat * d_gain)
        return value if side is None else value * flags_ref[1 + side].astype(F32)

    sources = ((grad_prev_ref, z_prev_ref), (grad_ref, z_ref), (grad_next_ref, z_next_ref))
    fill_frame(frame_ref, shape, padded, sources, make)
    span = rows * count * padded
    acc_ref[:, 0:8, :] = jnp.zeros((3, 8, acc_ref.shape[2]), F32)
    acc_ref[:, 8 + span :, :] = jnp.zeros((3, 8, acc_ref.shape[2]), F32)
    for kw in range(3):
        copies[kw].wait()
        for kh in range(3):
            start = (2 - kh) * count * padded
            part = dot_nt(frame_ref[start : start + span, :], w_buf[kw, kh])
            acc_ref[kw, 8 : 8 + span, :] = part if kh == 0 else acc_ref[kw, 8 : 8 + span, :] + part
    lanes = acc_ref.shape[2] // 128
    totals = [[None, None] for _ in range(lanes)]

    def finish(value, where, columns):
        hat = (z_in_ref[where, columns] - norm_in_ref[0:1, columns]) * norm_in_ref[1:2, columns]
        grad = gelu_slope(hat * gain_ref[layer, 0:1, columns] + bias_ref[layer, 0:1, columns]) * value
        keep = totals[columns.start // 128]
        for k, term in enumerate((grad, grad * hat)):
            keep[k] = fold(term) if keep[k] is None else keep[k] + fold(term)
        return grad

    shifted_sum(acc_ref, shape, padded, (1, 0, -1), pre_ref, finish)
    for j in range(lanes):
        put_copies(stat_ref, slice(j * 128, (j + 1) * 128), *totals[j])


def reduce_back_start(layer, total, grad_ref, z_ref, norm_ref, stack_ref, gain_ref, dz_ref, sums_ref):
    sums_ref[0:1, :] = fold(stack_ref[:, 0, :])
    sums_ref[1:2, :] = fold(stack_ref[:, 1, :])
    mean, scale = norm_ref[0:1, :], norm_ref[1:2, :]
    d_bias, d_gain = sums_ref[0:1, :] * (1.0 / total), sums_ref[1:2, :] * (1.0 / total)
    factor = gain_ref[layer, 0:1, :] * scale

    def step(rows, carry):
        hat = (z_ref[rows, :] - mean) * scale
        dz_ref[rows, :] = (factor * (grad_ref[rows, :] - d_bias - hat * d_gain)).astype(BF16)
        return carry

    row_loop(z_ref.shape[0], step, 0)


def reduce_back_kernel(
    layer, total, flags_ref, grad_ref, z_ref, norm_ref, stack_ref, gain_ref, w_ref, out_grad_ref,
    z_out_ref, u_ref, norm_out_ref, gain_out_ref, bias_out_ref,
    dz_ref, sums_ref, next_ref, kept_ref, sent_ref, w_buf, grad_buf, z_buf, u_buf, next_buf, part_ref, sems,
):
    cuts = blocks(out_grad_ref.shape[1])
    streams = [
        Stream(w_ref.at[layer], w_buf, cuts, sems.at[0], True),
        Stream(out_grad_ref, grad_buf, cuts, sems.at[1]),
        Stream(z_out_ref, z_buf, cuts, sems.at[2]),
        Stream(u_ref, u_buf, cuts, sems.at[3]),
    ]
    result = Stream(next_buf, next_ref, cuts, sems.at[4])
    fetch(streams)
    reduce_back_start(layer, total, grad_ref, z_ref, norm_ref, stack_ref, gain_ref, dz_ref, sums_ref)
    stats = []
    for i, c in enumerate(cuts):
        arrive(streams, i)
        part_ref[...] = dot_nt(dz_ref[...], w_buf[c, :])

        def slope(rows, carry, c=c):
            hat, pre = summed(z_buf, u_buf, norm_out_ref, gain_out_ref, bias_out_ref, layer - 1, rows, c)
            grad = gelu_slope(pre) * (grad_buf[rows, c] + part_ref[rows, :])
            next_buf[rows, c] = grad
            return carry[0] + grad, carry[1] + grad * hat

        zero = jnp.zeros((STEP, c.stop - c.start), F32)
        sums = row_loop(z_ref.shape[0], slope, (zero, zero))
        result.start(i)
        stats.append(jnp.concatenate([fold(s) for s in sums], 0))
    put_halves(flags_ref[0], jnp.concatenate(stats, 1), kept_ref, sent_ref)
    arrive_all(result, cuts)


def input_kernel(layer, total, grad_ref, z_ref, norm_ref, stack_ref, gain_ref, dz_ref, sums_ref):
    reduce_back_start(layer, total, grad_ref, z_ref, norm_ref, stack_ref, gain_ref, dz_ref, sums_ref)


def input_grad_kernel(layer, dz_ref, out_grad_ref, w_ref, next_ref, w_buf, grad_buf, next_buf, sems):
    cuts = blocks(out_grad_ref.shape[1])
    streams = [
        Stream(w_ref.at[layer], w_buf, cuts, sems.at[0], True),
        Stream(out_grad_ref, grad_buf, cuts, sems.at[1]),
    ]
    result = Stream(next_buf, next_ref, cuts, sems.at[2])
    fetch(streams)
    for i, c in enumerate(cuts):
        arrive(streams, i)
        next_buf[:, c] = grad_buf[:, c] + dot_nt(dz_ref[...], w_buf[c, :])
        result.start(i)
    arrive_all(result, cuts)


def store_halves(core, value_ref, axis, size, store):
    for which, bit in ((0, core), (1, 1 - core)):
        for x in range(value_ref.shape[axis] // (2 * size)):
            piece = pl.ds(pl.multiple_of((2 * x + bit) * size, 128), size)
            store(which, x, value_ref[piece, :] if axis == 0 else value_ref[:, piece])


def place(index):
    return index & 1, (index >> 1) & 1, index >> 2


def expand_outer_kernel(flags_ref, left_ref, right_ref, kept_ref, sent_ref, value_ref):
    outs = (kept_ref, sent_ref)
    for c in blocks(right_ref.shape[1]):
        value_ref[...] = dot_tn(left_ref[...], right_ref[:, c])

        def store(which, x, piece, c=c):
            piece = piece.astype(BF16)
            for at in range(0, piece.shape[1], 256):
                y, low, high = place((c.start + at) // 256)
                for half in range(2):
                    outs[which][x, y, low, high, half * 128 : (half + 1) * 128, :] = piece[
                        :, at + half * 128 : at + (half + 1) * 128
                    ]

        store_halves(flags_ref[0], value_ref, 0, 128, store)


def reduce_outer_kernel(flags_ref, left_ref, right_ref, kept_ref, sent_ref, value_ref):
    outs = (kept_ref, sent_ref)
    for c in blocks(left_ref.shape[1]):
        value_ref[...] = dot_tn(left_ref[:, c], right_ref[...])

        def store(which, x, piece, c=c):
            piece = piece.astype(BF16)
            for at in range(0, piece.shape[0], 256):
                outs[which][(x, *place((c.start + at) // 256))] = piece[at : at + 256, :]

        store_halves(flags_ref[0], value_ref, 1, 128, store)


def spatial_taps(shape, padded, grad_ref, frame_ref, line_ref, moved_ref, tap):
    count, rows, width = shape
    span = rows * count * padded
    start = count * padded
    line_ref[0:8, :] = jnp.zeros((8, line_ref.shape[1]), F32)
    line_ref[8 + span :, :] = jnp.zeros((8, line_ref.shape[1]), F32)
    line_ref[8 : 8 + span, :] = grad_ref[start : start + span, :].astype(F32)
    for kw in range(3):
        for b in range(0, span, padded):
            for c in range(0, line_ref.shape[1], 128):
                moved_ref[b : b + padded, c : c + 128] = line_ref[
                    8 + b + 1 - kw : 8 + b + 1 - kw + padded, c : c + 128
                ].astype(BF16)
        for kh in range(3):
            at = kh * count * padded
            tap(3 * kh + kw, dot_tn(moved_ref[...], frame_ref[at : at + span, :]))


def spatial_outer_kernel(
    shape, padded, flags_ref, grad_ref, frame_ref, kept_ref, sent_ref, line_ref, moved_ref, value_ref
):
    outs = (kept_ref, sent_ref)

    def tap(k, value):
        value_ref[...] = value

        def store(which, x, piece):
            piece = piece.astype(BF16)
            for at in range(0, piece.shape[0], 64):
                outs[which][(x, *place(at // 64), slice(k * 64, (k + 1) * 64))] = piece[at : at + 64, :]

        store_halves(flags_ref[0], value_ref, 1, 128, store)

    spatial_taps(shape, padded, grad_ref, frame_ref, line_ref, moved_ref, tap)


def spatial_plain_kernel(shape, padded, grad_ref, frame_ref, out_ref, line_ref, moved_ref):
    def tap(k, value):
        out_ref[k] = value.astype(BF16)

    spatial_taps(shape, padded, grad_ref, frame_ref, line_ref, moved_ref, tap)


def early_outer_kernel(cot_ref, state_ref, act_ref, dz_ref, out_ref, part_ref, sem):
    first = 0
    for left_ref, right_ref in ((cot_ref, state_ref), (act_ref, dz_ref)):
        height = left_ref.shape[1] // out_ref.shape[1]
        for a in blocks(left_ref.shape[1], height):
            for b in blocks(right_ref.shape[1]):
                value = dot_tn(left_ref[:, a], right_ref[:, b]).astype(BF16)
                for i in range(0, value.shape[0], height):
                    for j in range(0, value.shape[1], 128):
                        at = first + ((b.start + j) // 128 % 2) * height
                        part_ref[(b.start + j) // 256, (a.start + i) // height, at : at + height, :] = value[
                            i : i + height, j : j + 128
                        ]
        first += 2 * height
    copy = pltpu.make_async_copy(part_ref, out_ref.at[:, :, 0:first, :], sem.at[0])
    copy.start()
    copy.wait()


def early_spatial_kernel(
    shape, padded, grad_ref, frame_ref, held_ref, out_ref, line_ref, moved_ref, part_ref, sem
):
    def tap(k, value):
        for j in range(part_ref.shape[1]):
            columns = value[:, j * 128 : (j + 1) * 128].astype(BF16)
            for i in range(part_ref.shape[0]):
                part_ref[i, j, k * 64 : (k + 1) * 64, :] = columns[i * 64 : (i + 1) * 64, :]

    spatial_taps(shape, padded, grad_ref, frame_ref, line_ref, moved_ref, tap)
    rows = part_ref.shape[2]
    copy = pltpu.make_async_copy(part_ref, out_ref.at[:, :, out_ref.shape[2] - rows :, :], sem.at[0])
    copy.start()
    copy.wait()


def add_split_kernel(splits, flags_ref, *refs):
    refs = list(refs)
    outs = refs[-2 * len(splits) :]
    for n, (sources, flag, axis) in enumerate(splits):
        offset = 0
        for kept, got, first, rows in sources:
            lead = refs[kept].shape[:-2]
            others = [d for d in lead[:axis] + lead[axis + 1 :]]
            spots = [()]
            for d in others:
                spots = [spot + (i,) for spot in spots for i in range(d)]
            for which in range(2):
                index = flags_ref[flag] if which == 0 else 1 - flags_ref[flag]
                for spot in spots:
                    where = spot[:axis] + (index,) + spot[axis:] + (slice(first, first + rows), slice(None))
                    value = refs[kept][where].astype(F32) + refs[got][where].astype(F32)
                    outs[2 * n + which][spot + (slice(offset, offset + rows), slice(None))] = value.astype(BF16)
            offset += rows


def final_kernel(
    first_kept, first_got, last_kept, last_got, early_ref, one_0, two_0, one_1, two_1, out_0, out_1,
    reduce_ref, spatial_ref, expand_ref, heads_ref, gain_mid_ref, bias_mid_ref, gain_out_ref, bias_out_ref,
):
    def add(kept, got, start, rows):
        where = slice(start, start + rows)
        return kept[where, :].astype(F32) + got[where, :].astype(F32)

    high, wide = expand_ref.shape[1], spatial_ref.shape[2]
    taps_rows = spatial_ref.shape[1] * wide
    half = first_kept.shape[0] // 2
    for i in range(2):
        columns = slice(i * 128, (i + 1) * 128)
        expand_ref[0, :, columns] = add(first_kept, first_got, i * half, high)
        side = reduce_ref.shape[1] // 2
        for k, at in ((1, 2 * i * side), (0, (2 * i + 1) * side)):
            reduce_ref[k, i * side : (i + 1) * side, :] = add(last_kept, last_got, at, side)
    spatial = [add(first_kept, first_got, i * half + high, half - high) for i in range(2)]
    heads = heads_ref.shape[0]
    spatial = (jnp.concatenate(spatial, 0), early_ref[2 * heads + 2 * high :, :].astype(F32))
    for k in range(2):
        for tap in range(taps_rows // wide):
            spatial_ref[k, tap] = spatial[k][tap * wide : (tap + 1) * wide]
    for i in range(2):
        heads_ref[:, i * 128 : (i + 1) * 128] = early_ref[i * heads : (i + 1) * heads, :].astype(F32)
        at = 2 * heads + i * high
        expand_ref[1, :, i * 128 : (i + 1) * 128] = early_ref[at : at + high, :].astype(F32)
    for k, (one, two, out) in enumerate(((one_0, two_0, out_0), (one_1, two_1, out_1))):
        for j, sums in enumerate((one, two)):
            bias_mid_ref[k, j : j + 1, :] = sums[0:1, :]
            gain_mid_ref[k, j : j + 1, :] = sums[1:2, :]
        bias_out_ref[k : k + 1, :] = out[0:1, :]
        gain_out_ref[k : k + 1, :] = out[1:2, :]


def shaped(shape, dtype=F32):
    return jax.ShapeDtypeStruct(shape, dtype)


KINDS = {
    "v": pl.BlockSpec(memory_space=pltpu.VMEM),
    "h": pl.BlockSpec(memory_space=pltpu.HBM),
    "s": pl.BlockSpec(memory_space=pltpu.SMEM),
}


def call(name, kernel, specs, args, out_specs, outs, scratch=(), sems=None, flops=0, aliases=None, limit=VMEM_LIMIT):
    nbytes = sum(math.prod(o.shape) * o.dtype.itemsize for o in outs)
    return pl.pallas_call(
        kernel,
        out_shape=outs,
        in_specs=[KINDS[s] for s in specs],
        out_specs=[KINDS[s] for s in out_specs],
        scratch_shapes=[pltpu.VMEM(s.shape, s.dtype) for s in scratch]
        + ([] if sems is None else [pltpu.SemaphoreType.DMA(sems)]),
        compiler_params=pltpu.CompilerParams(vmem_limit_bytes=limit),
        cost_estimate=pl.CostEstimate(flops=1, bytes_accessed=1, transcendentals=0),
        input_output_aliases=aliases or {},
        name=name,
    )(*args)


def spread(copies, groups=None):
    return lax.all_to_all(copies, BOTH, 0, 0, tiled=True, axis_index_groups=groups)


def merge_moments(stack):
    means, squares = stack[:, 0], stack[:, 1]
    mean = jnp.mean(means, 0)
    off = means - mean
    return jnp.stack([mean, jnp.mean(squares, 0) + jnp.mean(off * off, 0)])


def merge_sums(stack):
    return jnp.sum(stack, 0)


def share_halves(kept, sent, merge):
    devices, cores = lax.axis_size(BOTH), lax.axis_size("ba")
    swap = [(i, i ^ 1) for i in range(cores)]
    pair = merge(jnp.stack([kept, lax.ppermute(sent, "ba", swap)]))
    groups = [list(range(c, devices, 2)) for c in range(2)]
    own = merge(spread(jnp.broadcast_to(pair[None], (devices // 2,) + pair.shape), groups))
    return own, lax.ppermute(own, "ba", swap)


def neighbours(first, last):
    devices = lax.axis_size("ha")
    up = [(i, i + 1) for i in range(devices - 1)]
    down = [(j, i) for i, j in up]
    return lax.ppermute(last, "ha", up), lax.ppermute(first, "ha", down)


def swap(x, axis, bit):
    return lax.ppermute(x, axis, [(i, i ^ bit) for i in range(lax.axis_size(axis))])


CORE, LOW_X, Y, LOW_Z, HIGH_Z = 0, 5, 6, 7, 8


def add_split(name, flags, arrays, splits):
    outs = []
    for sources, _, axis in splits:
        lead = arrays[sources[0][0]].shape[:-2]
        shape = lead[:axis] + lead[axis + 1 :] + (sum(rows for *_, rows in sources), 128)
        outs += [shaped(shape, BF16)] * 2
    return call(
        name, functools.partial(add_split_kernel, splits), "s" + "v" * len(arrays), [flags, *arrays],
        "v" * len(outs), outs, limit=SMALL_LIMIT,
    )


class Moving:
    def __init__(self, name, flags, pairs):
        self.name, self.flags = name, flags
        self.rows = [kept.shape[-2] for kept, _ in pairs]
        self.kept = [kept for kept, _ in pairs]
        self.got = [swap(sent, "ba", 1) for _, sent in pairs]
        self.stage = 0

    def state(self):
        return self.kept

    def put(self, state):
        self.kept = state

    def advance(self):
        arrays = []
        for kept, got in zip(self.kept, self.got):
            arrays += [kept, got]
        name = f"sum_{self.name}_{self.stage}"
        if self.stage == 0:
            halves = [rows // 2 for rows in self.rows]
            splits = [
                ([(2 * i, 2 * i + 1, 0, half) for i, half in enumerate(halves)], LOW_X, 0),
                ([(2 * i, 2 * i + 1, half, half) for i, half in enumerate(halves)], Y, 1),
            ]
        elif self.stage == 1:
            rows = [x.shape[-2] for x in self.kept]
            splits = [([(0, 1, 0, rows[0])], Y, 0), ([(2, 3, 0, rows[1])], LOW_X, 0)]
        elif self.stage == 2:
            splits = [([(2 * i, 2 * i + 1, 0, x.shape[-2]) for i, x in enumerate(self.kept)], LOW_Z, 0)]
        else:
            splits = [([(0, 1, 0, self.kept[0].shape[-2])], HIGH_Z, 0)]
        outs = add_split(name, self.flags, arrays, splits)
        moves = [[("ba", 2), ("ha", 1)], [("ha", 1), ("ba", 2)], [("ha", 2)], [("ha", 4)]][self.stage]
        self.kept = list(outs[0::2])
        self.got = [swap(x, *move) for x, move in zip(outs[1::2], moves)]
        self.stage += 1


def tie(along, moving):
    along, states = lax.optimization_barrier((along, [one.state() for one in moving]))
    for one, state in zip(moving, states):
        one.put(state)
    return along


def scatter_plain(x, row_axis, column_axis):
    for axis in ("ha", "ba"):
        x = lax.psum_scatter(x, axis, scatter_dimension=1 if axis == row_axis else 2, tiled=True)
    return x.astype(F32)


def body(
    images, w_reduce, w_spatial, w_expand, gain_mid, bias_mid, gain_out, bias_out, w_heads, targets, thresholds
):
    count, rows, width, chans = images.shape
    shape = (count, rows, width)
    padded = (width // 16 + 1) * 16
    pixels = count * rows * width
    total = pixels * lax.axis_size(BOTH)
    mid = w_reduce.shape[2]
    head_columns = w_heads.shape[1]
    frame_rows, span = (rows + 2) * count * padded, rows * count * padded
    edge = shaped((count * padded, mid), BF16)
    here, last_row, across = lax.axis_index("ha"), lax.axis_size("ha") - 1, lax.axis_size("ba")
    column = lax.axis_index("ba")
    flags = jnp.stack(
        [
            column % 2, here > 0, here < last_row,
            jnp.maximum(here - 1, 0) * across + column, jnp.minimum(here + 1, last_row) * across + column,
            column // 2 % 2, here % 2, here // 2 % 2, here // 4 % 2,
        ]
    ).astype(jnp.int32)
    cuts = len(blocks(chans))
    stats_mid = shaped((lax.axis_size(BOTH), 2, mid))
    pair_mid, norm_mid, pair_out = shaped((2, mid)), shaped((4, mid)), shaped((2, chans))
    half_out = shaped((2, chans // 2))
    mids, outs_f = shaped((pixels, mid)), shaped((pixels, chans))
    mids_b, outs_b = shaped((pixels, mid), BF16), shaped((pixels, chans), BF16)
    w_one, w_three, w_two = shaped((chans, mid), BF16), shaped((mid, chans), BF16), shaped((3, 3, mid, mid), BF16)
    acc_two = shaped((3, span + 16, mid))
    block = shaped((pixels, min(BLOCK, chans)))
    small = 2 * pixels * chans * mid

    state = images.reshape(pixels, chans)
    kept = []
    z_one, stat, first, last = call(
        "reduce_0", functools.partial(reduce_kernel, 0, shape, padded), "hh", (state, w_reduce),
        "vvvv", [mids, stats_mid, edge, edge], [outs_b, w_one], (2, cuts), small,
    )
    for layer in range(2):
        prev, after = neighbours(first, last)
        stack = spread(stat)
        frame, z_two, stat, norm_one, *z_two_edges = call(
            f"spatial_{layer}", functools.partial(spatial_kernel, layer, shape, padded), "svvvvvvh",
            (flags, z_one, prev, after, stack, gain_mid, bias_mid, w_spatial),
            "vvvvvv", [shaped((frame_rows, mid), BF16), mids, stats_mid, norm_mid, edge, edge],
            [w_two, acc_two], (3,), 10 * small // 4,
        )
        stack = spread(stat)
        act_two, z_three, keep, send, norm_two = call(
            f"expand_{layer}", functools.partial(expand_kernel, layer), "svvvvh",
            (flags, z_two, stack, gain_mid, bias_mid, w_expand),
            "vhvvv", [mids_b, outs_f, half_out, half_out, norm_mid], [w_three, outs_f], (2, cuts), small,
        )
        own, other = share_halves(keep, send, merge_moments)
        saved = dict(
            inputs=state, z_one=z_one, norm_one=norm_one, frame=frame, z_two=z_two, z_two_edges=z_two_edges,
            norm_two=norm_two, act_two=act_two, z_three=z_three,
        )
        kept.append(saved)
        if layer == 0:
            state, z_one, stat, first, last, saved["norm_three"] = call(
                "join", functools.partial(join_kernel, 0, shape, padded), "shhvvvvh",
                (flags, z_three, state, own, other, gain_out, bias_out, w_reduce),
                "hvvvvv", [outs_b, mids, stats_mid, edge, edge, pair_out],
                [w_one, outs_f, outs_b, outs_b], (4, cuts), small,
            )
    (own, other), edge_rows = lax.optimization_barrier(((own, other), [k["z_two_edges"] for k in kept]))
    edge_rows = neighbours(*(jnp.stack(rows) for rows in zip(*edge_rows)))
    for i, k in enumerate(kept):
        k["z_two_edges"] = [rows[i] for rows in edge_rows]
    wanted = targets.reshape(pixels, head_columns)
    level = thresholds.reshape(pixels, 1).astype(F32) * 0.001
    heads_wide = shaped((pixels, head_columns))
    state, cot, grad, keep, send, kept[1]["norm_three"] = call(
        "heads", functools.partial(heads_kernel, 1, total), "shhvvvvhhv",
        (flags, z_three, state, own, other, gain_out, bias_out, w_heads, wanted, level),
        "hvhvvv", [outs_b, shaped((pixels, head_columns), BF16), outs_f, half_out, half_out, pair_out],
        [
            shaped((chans, head_columns), BF16), outs_f, outs_b, shaped((pixels, head_columns), jnp.int32),
            outs_b, outs_f, heads_wide, shaped((3,) + block.shape),
        ],
        (6, cuts), 3 * small,
    )
    (keep, send), edge_rows = lax.optimization_barrier(((keep, send), [k["z_two_edges"] for k in kept]))
    for k, pair in zip(kept, edge_rows):
        k["z_two_edges"] = pair
    activations = state
    fast = across == 4 and last_row == 7 and mid == 512 and chans == 2048 and head_columns % 64 == 0
    parts_out = lambda rows: [shaped((2, 2, 2, 2, rows, 128), BF16)] * 2
    square = shaped((mid, mid))

    moving, reduce_pairs = [], []
    reduce_grads, spatial_grads, expand_grads = [None, None], [None, None], [None, None]
    mid_sums, out_sums = [None, None], [None, None]
    for layer in (1, 0):
        k = kept[layer]
        own, other = share_halves(keep, send, merge_sums)
        if fast and layer == 0:
            (own, other), reduce_pairs = lax.optimization_barrier(((own, other), reduce_pairs))
        dz_three, pre_two, stat, out_sums[layer], first, last = call(
            f"expand_back_{layer}", functools.partial(expand_back_kernel, layer, total, shape, padded), "shhvvvvvvvvh",
            (flags, grad, k["z_three"], k["norm_three"], own, other, gain_out, k["z_two"], k["norm_two"], gain_mid, bias_mid, w_expand),
            "hvvvvv", [outs_b, mids, stats_mid, pair_out, edge, edge],
            [w_three, outs_f, outs_f, outs_b, mids], (4, cuts), small,
        )
        grad_prev, grad_next = neighbours(first, last)
        stack = spread(stat)
        if not fast:
            expand_grads[layer] = scatter_plain(dot_tn(k["act_two"], dz_three).astype(BF16)[None], "ba", "ha")[0]
            if layer == 1:
                grad_heads = scatter_plain(dot_tn(cot, activations).astype(BF16)[None], "ba", "ha")[0].T
        elif layer == 1:
            rows_early = (2 * head_columns + 2 * mid) // across
            rows_all = rows_early + 9 * mid // (last_row + 1)
            early = call(
                "outer_early", early_outer_kernel, "vvvv", (cot, activations, k["act_two"], dz_three), "h",
                [shaped((last_row + 1, across, rows_all, 128), BF16)],
                [shaped((last_row + 1, across, rows_early, 128), BF16)], (1,), 3 * small,
            )[0]
            stack, early = lax.optimization_barrier((stack, early))
        else:
            expand_pair = call(
                "outer_expand", expand_outer_kernel, "svv", (flags, k["act_two"], dz_three), "vv", parts_out(256),
                [square], flops=small,
            )
            stack, expand_pair = lax.optimization_barrier((stack, expand_pair))
        frame, pre_one, stat, sums_two = call(
            f"spatial_back_{layer}", functools.partial(spatial_back_kernel, layer, total, shape, padded), "svvvvvvvvvvvvh",
            (flags, pre_two, grad_prev, grad_next, k["z_two"], *k["z_two_edges"], k["norm_two"], stack, gain_mid, bias_mid, k["z_one"], k["norm_one"], w_spatial),
            "vvvv", [shaped((frame_rows, mid), BF16), mids, stats_mid, pair_mid], [w_two, acc_two], (3,), 10 * small // 4,
        )
        stack = spread(stat)
        line, moved = shaped((span + 16, mid)), shaped((span, mid), BF16)
        if fast and layer == 1:
            early = call(
                "outer_spatial_1", functools.partial(early_spatial_kernel, shape, padded), "vvh",
                (frame, k["frame"], early), "h", [shaped(early.shape, BF16)],
                [line, moved, shaped((last_row + 1, across, 9 * mid // (last_row + 1), 128), BF16)], (1,),
                10 * small // 4, {2: 0},
            )[0]
            stack, early = lax.optimization_barrier((stack, early))
            early = early.reshape((-1,) + early.shape[2:])
            early = lax.psum_scatter(early, BOTH, scatter_dimension=0, tiled=True)[0]
        elif fast:
            spatial_pair = call(
                f"outer_spatial_{layer}", functools.partial(spatial_outer_kernel, shape, padded), "svv",
                (flags, frame, k["frame"]), "vv", parts_out(9 * 64), [line, moved, square], flops=10 * small // 4,
            )
        else:
            x = call(
                f"outer_spatial_{layer}", functools.partial(spatial_plain_kernel, shape, padded), "vv",
                (frame, k["frame"]), "v", [shaped((9, mid, mid), BF16)], [line, moved], flops=10 * small // 4,
            )[0]
            spatial_grads[layer] = scatter_plain(x, "ha", "ba")
        if layer == 1:
            b = kept[0]
            dz_one, sums_one, grad, keep, send = call(
                "reduce_back_1", functools.partial(reduce_back_kernel, 1, total), "svvvvvhhhhvvv",
                (flags, pre_one, k["z_one"], k["norm_one"], stack, gain_mid, w_reduce, grad, b["z_three"], b["inputs"], b["norm_three"], gain_out, bias_out),
                "vvhvv", [mids_b, pair_mid, outs_f, half_out, half_out],
                [w_one, outs_f, outs_f, outs_b, outs_f, block], (5, cuts), small,
            )
        else:
            if fast:
                moving.append(Moving("early", flags, [expand_pair, spatial_pair]))
                moving[0].advance()
                stack = tie(stack, moving)
            dz_one, sums_one = call(
                "reduce_back_0", functools.partial(input_kernel, 0, total), "vvvvv",
                (pre_one, k["z_one"], k["norm_one"], stack, gain_mid), "vv", [mids_b, pair_mid],
            )
        if fast:
            reduce_pair = call(
                f"outer_reduce_{layer}", reduce_outer_kernel, "svv", (flags, k["inputs"], dz_one), "vv", parts_out(256),
                [square], flops=small,
            )
            reduce_pairs.append(reduce_pair)
            if layer == 0:
                moving.append(Moving("last", flags, reduce_pairs))
                moving[1].advance()
        else:
            reduce_grads[layer] = scatter_plain(dot_tn(k["inputs"], dz_one).astype(BF16)[None], "ha", "ba")[0]
        mid_sums[layer] = [sums_one, sums_two]
    input_grad = call(
        "input_grad", functools.partial(input_grad_kernel, 0), "vhh", (dz_one, grad, w_reduce),
        "h", [outs_f], [w_one, outs_f, outs_f], (3, cuts), small,
    )[0]
    if fast:
        first, last = moving
        first.got, input_grad = tie((first.got, input_grad), [last])
        while last.stage < 4:
            first.advance()
            last.got = tie(last.got, [first])
            last.advance()
            first.got = tie(first.got, [last])
        tile_in, tile_out = mid // (last_row + 1), mid // across
        grad_reduce, grad_spatial, grad_expand, grad_heads, gain_mids, bias_mids, gain_outs, bias_outs = call(
            "final", final_kernel, "v" * 11,
            (first.kept[0], first.got[0], last.kept[0], last.got[0], early, *mid_sums[0], *mid_sums[1], *out_sums),
            "v" * 8,
            [
                shaped((2, chans // (last_row + 1), tile_out)), shaped((2, 9, tile_in, tile_out)),
                shaped((2, tile_out, chans // (last_row + 1))), shaped((head_columns // across, chans // (last_row + 1))),
                shaped((2, 2, mid)), shaped((2, 2, mid)), shaped((2, chans)), shaped((2, chans)),
            ],
            limit=SMALL_LIMIT,
        )
        grad_spatial, grad_heads = jnp.swapaxes(grad_spatial, 2, 3), grad_heads.T
    else:
        grad_reduce, grad_expand = jnp.stack(reduce_grads), jnp.stack(expand_grads)
        grad_spatial = jnp.swapaxes(jnp.stack(spatial_grads), 2, 3)
        mids_all, outs_all = jnp.stack([jnp.stack(pair) for pair in mid_sums]), jnp.stack(out_sums)
        gain_mids, bias_mids = mids_all[:, :, 1], mids_all[:, :, 0]
        gain_outs, bias_outs = outs_all[:, 1], outs_all[:, 0]
    return (
        activations.reshape(images.shape),
        input_grad.reshape(images.shape),
        grad_reduce,
        grad_spatial.reshape((2, 3, 3) + grad_spatial.shape[2:]),
        grad_expand,
        gain_mids,
        bias_mids,
        gain_outs,
        bias_outs,
        grad_heads,
    )


def solution(mesh):
    pixels = P("ba", "ha", None, None)
    return jax.shard_map(
        body,
        mesh=mesh,
        in_specs=(pixels, P(), P(), P(), P(), P(), P(), P(), P(), pixels, P("ba", "ha", None)),
        out_specs=(
            pixels,
            pixels,
            P(None, "ha", "ba"),
            P(None, None, None, "ba", "ha"),
            P(None, "ba", "ha"),
            P(),
            P(),
            P(),
            P(),
            P("ha", "ba"),
        ),
        check_vma=False,
    )
```
